128 devices in a mesh: dp: 32 (over y, z, core), tensor: 4 (over x).
Axes of the slice: x: 4, y: 4, z: 4, core: 2. Of those that a mesh axis runs over, the one named last changes fastest.
Arguments:
- gradient: bfloat16 [4, 1, 512, 16384], P('tensor', None, 'dp'), may hold values from -6 to 6
- slot_block: int32 [4, 64], P('tensor'), may hold values from -1 to 31, as said below
- refresh_target: int32 [256], replicated, may hold values from -1 to 127, as said below
- first_moment: float32 [4, 64, 512, 512], P('tensor', 'dp'), may hold values from -6 to 6
- second_moment: float32 [4, 64, 512, 512], P('tensor', 'dp'), may hold values from 0.1 to 2
- left_gram: float32 [4, 64, 512, 512], P('tensor', 'dp'), as said below
- right_gram: float32 [4, 64, 512, 512], P('tensor', 'dp'), as said below
- left_basis: float32 [4, 64, 512, 512], P('tensor', 'dp'), as said below
- right_basis: float32 [4, 64, 512, 512], P('tensor', 'dp'), as said below
Outputs:
- update: float32 [4, 64, 512, 512], P('tensor', 'dp')
- new_left_basis: float32 [4, 64, 512, 512], P('tensor', 'dp')
- new_right_basis: float32 [4, 64, 512, 512], P('tensor', 'dp')
The draws below stay inside these ranges and needn't reach their ends.
Inputs may be any that keep to these rules, and one draw needn't show every extreme that they name: `slot_block`: blocks of a tensor index are numbered r * 32 + c; each of the 32 blocks is held by exactly one slot of that tensor index, -1 marks an empty slot. An owner's blocks fill its first slots; 16 owners of each tensor index hold blocks, all of them but at most one in all 2 slots, the other owners none. `refresh_target`: entry (g * 4 + t) * 2 + s belongs to slot s of the device at dp index g and tensor index t. It is -1, or h * 4 + u for the device at dp index h and tensor index u that refreshes that slot. Exactly 32 entries are not -1; they lie in slots that hold a block and name distinct devices that hold no block. The last device holds no block and is always named. `left_gram`: each matrix is symmetric positive definite. `right_gram`: each matrix is symmetric positive definite. `left_basis`: each matrix is invertible. `right_basis`: each matrix is invertible.
All inputs are finite; a program needn't handle non-finite values.
Results may differ from the reference program's by a relative error of at most 0.0003.
Values may be sent and summed in bfloat16 or wider, within the bound.
No kernel may reach another device: no remote copies, remote signals or barrier semaphores. Data moves between devices by JAX's collectives and lax.ppermute only.
A program may use at most 128 MiB of HBM per device.

```python
import math
import jax
import jax.numpy as jnp
from jax import lax

D = 16384
BLK = 512
RB = 1
SWEEPS = 2
NBT = 32
SLOTS = 2
NFULL = 16
NREF = 32
N_DP = 32
N_TENSOR = 4


def tables(key):
    keys = jax.random.split(key, 5)
    free_order = jax.vmap(lambda one_key: jax.random.permutation(one_key, N_DP))(jax.random.split(keys[0], N_TENSOR)).astype(jnp.int32)
    last_order = jnp.concatenate([jax.random.permutation(keys[4], N_DP - 1).astype(jnp.int32), jnp.full((1,), N_DP - 1, jnp.int32)])
    owner_order = jnp.concatenate([free_order[:N_TENSOR - 1], last_order[None, :]], axis=0)
    rank = jnp.argsort(owner_order.astype(jnp.int32), axis=1).astype(jnp.int32)
    block_order = jax.vmap(lambda one_key: jax.random.permutation(one_key, NBT))(jax.random.split(keys[1], N_TENSOR)).astype(jnp.int32)
    place = rank[:, :, None] * SLOTS + jnp.arange(SLOTS, dtype=jnp.int32)[None, None, :]
    clipped = jnp.minimum(place, NBT - 1).reshape(N_TENSOR, N_DP * SLOTS)
    held = jnp.take_along_axis(block_order, clipped, axis=1).reshape(N_TENSOR, N_DP, SLOTS)
    held = jnp.where(place < NBT, held, -1).astype(jnp.int32)
    slot_table = held.reshape(N_TENSOR, N_DP * SLOTS)
    by_device = jnp.transpose(held, (1, 0, 2)).reshape(-1)
    slot_score = jax.random.permutation(keys[2], N_DP * N_TENSOR * SLOTS).astype(jnp.int32)
    slot_score = jnp.where(by_device >= 0, slot_score, -1)
    chosen = lax.top_k(slot_score, NREF)[1]
    empty_device = jnp.transpose(rank >= NFULL).reshape(-1)
    device_score = jax.random.permutation(keys[3], N_DP * N_TENSOR).astype(jnp.int32)
    device_score = jnp.where(empty_device, device_score, -1)
    device_score = device_score.at[N_DP * N_TENSOR - 1].set(N_DP * N_TENSOR)
    helpers = lax.top_k(device_score, NREF)[1].astype(jnp.int32)
    target = jnp.full((N_DP * N_TENSOR * SLOTS,), -1, jnp.int32).at[chosen].set(helpers)
    return (slot_table, target)


def draw_slot_block(key, part):
    return tables(key)[0]


def draw_refresh_target(key, part):
    return tables(key)[1]


def definite(scale_key, noise, top):
    shape = noise.shape
    scales = jnp.exp(jax.random.uniform(scale_key, shape[:-1], jnp.float32, 0.0, jnp.log(top)))
    spread = 8.0 * (noise + jnp.swapaxes(noise, -1, -2)) / jnp.sqrt(2.0)
    identity = jnp.eye(shape[-1], dtype=jnp.float32)
    return spread + BLK * scales[..., None] * identity


def draw_left_gram(key, part):
    key = jax.random.fold_in(key, 11)
    scale_key, noise_key = jax.random.split(key)
    shape = (N_TENSOR, N_DP * SLOTS, BLK, BLK)
    noise = jax.random.normal(noise_key, shape, jnp.float32)
    top = 4.0
    return definite(scale_key, noise, top)


def draw_right_gram(key, part):
    key = jax.random.fold_in(key, 23)
    scale_key, noise_key = jax.random.split(key)
    shape = (N_TENSOR, N_DP * SLOTS, BLK, BLK)
    noise = jax.random.normal(noise_key, shape, jnp.float32)
    top = 4.0
    return definite(scale_key, noise, top)


def near_identity(noise):
    identity = jnp.eye(BLK, dtype=jnp.float32)
    return identity + 0.5 * noise / jnp.sqrt(float(BLK))


def draw_left_basis(key, part):
    key = jax.random.fold_in(key, 37)
    shape = (N_TENSOR, N_DP * SLOTS, BLK, BLK)
    noise = jax.random.normal(key, shape, jnp.float32)
    return near_identity(noise)


def draw_right_basis(key, part):
    key = jax.random.fold_in(key, 41)
    shape = (N_TENSOR, N_DP * SLOTS, BLK, BLK)
    noise = jax.random.normal(key, shape, jnp.float32)
    return near_identity(noise)


def block_levels(rng, shape, shards, smallest, top_value):
    def one(dim, blocks):
        heights = jax.random.uniform(jax.random.fold_in(jax.random.fold_in(rng, 6), dim), (blocks,), jnp.float32, smallest / len(shards), top_value / len(shards))
        return jnp.repeat(jnp.exp(heights), shape[dim] // blocks).reshape((-1,) + (1,) * (len(shape) - dim - 1))

    factor_of = one(*shards[0])
    for cut in shards[1:]:
        factor_of = factor_of * one(*cut)
    return factor_of


def bell_draw(key, dims, width, limit, cuts=(), kind=jnp.bfloat16):
    loudness = block_levels(key, dims, cuts, -0.22, 0.18) if cuts else 1.0
    drawn = jax.random.normal(key, dims, jnp.float32) * width * loudness
    return jnp.minimum(jnp.maximum(drawn, -limit), limit).astype(kind)


def setup_inputs(seed: int = 0) -> dict:
    streams_of = jax.random.split(jax.random.key(seed), 10)
    return {
        "gradient": bell_draw(streams_of[0], (N_TENSOR, RB, BLK, D), 1.0, 6.0, ((0, 4), (2, 32))),
        "slot_block": draw_slot_block(jax.random.fold_in(streams_of[9], 71), 0),
        "refresh_target": draw_refresh_target(jax.random.fold_in(streams_of[9], 71), 0),
        "first_moment": bell_draw(streams_of[3], (N_TENSOR, N_DP * SLOTS, BLK, BLK), 1.0, 6.0, ((0, 4), (1, 32)), jnp.float32),
        "second_moment": jnp.clip(jnp.exp(math.log(2.0) - 2.9957323 * jax.random.uniform(streams_of[4], (N_TENSOR, N_DP * SLOTS, BLK, BLK), jnp.float32) ** block_levels(streams_of[4], (N_TENSOR, N_DP * SLOTS, BLK, BLK), ((0, 4), (1, 32)), -0.2, 0.2)), 0.1, 2.0),
        "left_gram": draw_left_gram(jax.random.fold_in(streams_of[9], 71), 0),
        "right_gram": draw_right_gram(jax.random.fold_in(streams_of[9], 71), 0),
        "left_basis": draw_left_basis(jax.random.fold_in(streams_of[9], 71), 0),
        "right_basis": draw_right_basis(jax.random.fold_in(streams_of[9], 71), 0),
    }


highest = lax.Precision.HIGHEST

def orthonormal(gram_matrix, basis):
    for sweep_index in range(SWEEPS):
        image = jnp.dot(gram_matrix, basis, precision=highest)
        inner = jnp.dot(image.T, image, precision=highest)
        factor = jnp.linalg.cholesky(inner)
        basis = lax.linalg.triangular_solve(factor, image, left_side=False, lower=True, transpose_a=True)
    return basis

def reference(gradient, slot_block, refresh_target, first_moment, second_moment, left_gram, right_gram, left_basis, right_basis):
    per_row = N_DP * SLOTS
    columns = D // BLK

    def one_slot(index):
        tensor_index = index // per_row
        within = index % per_row
        owner = within // SLOTS
        position = within % SLOTS
        block_id = slot_block[tensor_index, within]
        safe_id = jnp.maximum(block_id, 0)
        anchor = jnp.zeros((), jnp.int32)
        start = (safe_id % columns * BLK).astype(jnp.int32)
        piece = lax.dynamic_slice(gradient, (tensor_index, (safe_id // columns).astype(jnp.int32), anchor, start), (1, 1, BLK, BLK))[0, 0]
        held = block_id >= 0
        wide = jnp.where(held, piece, jnp.zeros_like(piece)).astype(jnp.float32)
        left_new = 0.95 * left_gram[tensor_index, within] + 0.05 * jnp.dot(wide, wide.T, precision=highest)
        right_new = 0.95 * right_gram[tensor_index, within] + 0.05 * jnp.dot(wide.T, wide, precision=highest)
        left_old = left_basis[tensor_index, within]
        right_old = right_basis[tensor_index, within]
        rotated = jnp.dot(jnp.dot(left_old.T, wide, precision=highest), right_old, precision=highest)
        moment = 0.9 * first_moment[tensor_index, within] + 0.1 * rotated
        second = 0.95 * second_moment[tensor_index, within] + 0.05 * rotated * rotated
        normed = moment / (jnp.sqrt(second) + 1e-08)
        update = jnp.dot(jnp.dot(left_old, normed, precision=highest), right_old.T, precision=highest)
        update = jnp.where(held, update, jnp.zeros_like(update))
        refreshed = refresh_target[(owner * N_TENSOR + tensor_index) * SLOTS + position] >= 0
        fresh_left = jnp.where(refreshed, orthonormal(left_new, left_old), left_old)
        fresh_right = jnp.where(refreshed, orthonormal(right_new, right_old), right_old)
        return (update, fresh_left, fresh_right)
    results = lax.map(one_slot, jnp.arange(N_TENSOR * per_row, dtype=jnp.int32))
    shape = (N_TENSOR, per_row, BLK, BLK)
    return (results[0].reshape(shape), results[1].reshape(shape), results[2].reshape(shape))
```

```python
import functools

import jax
import jax.numpy as jnp
from jax import lax
from jax.experimental import pallas as pl
from jax.experimental.pallas import tpu as pltpu
from jax.sharding import PartitionSpec as P

BLOCK = 512
PANEL = 128
LEAF = 32
SLOTS = 2
MATS = 2 * SLOTS
CHUNK = 256
WORST = 17.0

f32 = jnp.float32
bf16 = jnp.bfloat16

NN = (((1,), (0,)), ((), ()))
NT = (((1,), (1,)), ((), ()))
TN = (((0,), (0,)), ((), ()))


def split(x):
    high = x.astype(bf16)
    return high, (x - high.astype(f32)).astype(bf16)


def dot(a, b, dims=NN):
    return lax.dot_general(a, b, dims, preferred_element_type=f32)


def dot3(a, b, dims=NN):
    return dot(a[0], b[0], dims) + (dot(a[0], b[1], dims) + dot(a[1], b[0], dims))


def unit_rows(x):
    return x * lax.rsqrt(jnp.sum(x * x, axis=1, keepdims=True))


def leaf(tiles):
    lane = lax.broadcasted_iota(jnp.int32, (8, 128), 1)
    row = lax.broadcasted_iota(jnp.int32, (8, 128), 0)
    within = lane % LEAF
    base = lane - within
    worst = jnp.zeros((1, 128), f32)
    tiles = list(tiles)
    for j in range(LEAF):
        t0, r0 = divmod(j, 8)
        source = base + j
        columns = [None] * t0 + [jnp.take_along_axis(tiles[t], source, axis=1) for t in range(t0, LEAF // 8)]
        inverse = lax.rsqrt(columns[t0][r0 : r0 + 1, :])
        worst = jnp.maximum(worst, jnp.where(inverse < WORST, 0.0, 1.0))
        pivot_row = tiles[t0][r0 : r0 + 1, :] + jnp.where(within[:1] == j, 1.0, 0.0)
        scaled = pivot_row * inverse
        for t in range(t0, LEAF // 8):
            factor = columns[t] * inverse
            if t == t0:
                factor = jnp.where(row > r0, factor, 0.0)
            tiles[t] = tiles[t] - factor * scaled
        own = jnp.where(within[:1] == j, inverse, scaled)
        tiles[t0] = jnp.where(row == r0, own, tiles[t0])
    for t in range(LEAF // 8):
        tiles[t] = jnp.where(within <= row + 8 * t, tiles[t], 0.0)
    return tiles, worst


def factor_panels(work, worst_ref):
    lane = lax.broadcasted_iota(jnp.int32, (LEAF, PANEL), 1)
    row = lax.broadcasted_iota(jnp.int32, (LEAF, PANEL), 0)
    for b in range(PANEL // LEAF):
        top = b * LEAF
        rows = slice(top, top + LEAF)
        packed = jnp.concatenate([work[m, rows, rows] for m in range(MATS)], axis=1)
        tiles, worst = leaf([packed[8 * t : 8 * t + 8] for t in range(LEAF // 8)])
        worst_ref[...] = jnp.maximum(worst_ref[...], worst)
        packed = jnp.concatenate(tiles, axis=0)
        below = PANEL - top - LEAF
        for m in range(MATS):
            inverse = split(packed[:, m * LEAF : (m + 1) * LEAF])
            band = jnp.where(lane - top == row, 1.0, jnp.where((lane >= top) & (lane < top + LEAF), 0.0, work[m, rows, :]))
            band = dot3(inverse, split(band))
            if below:
                under = slice(top + LEAF, PANEL)
                old = work[m, under, :]
                factor = dot3(split(old[:, rows]), inverse, NT)
                wide_lane = lax.broadcasted_iota(jnp.int32, (below, PANEL), 1)
                kept = jnp.where((wide_lane >= top) & (wide_lane < top + LEAF), 0.0, old)
                work[m, under, :] = kept - dot3(split(factor), split(band))
            work[m, rows, :] = band
    full_lane = lax.broadcasted_iota(jnp.int32, (PANEL, PANEL), 1)
    full_row = lax.broadcasted_iota(jnp.int32, (PANEL, PANEL), 0)
    for m in range(MATS):
        work[m] = jnp.where(full_lane <= full_row, work[m], 0.0)


def orthonormal_rows(z, work, worst_ref):
    for p in range(BLOCK // PANEL):
        rows = pl.ds(p * PANEL, PANEL)

        @pl.loop(0, MATS)
        def _(m):
            part = split(z[m, rows, :])
            work[m] = dot3(part, part, NT)

        factor_panels(work, worst_ref)

        @pl.loop(0, MATS)
        def _(m):
            fresh = dot3(split(work[m]), split(z[m, rows, :]))
            z[m, rows, :] = fresh
            if p + 1 < BLOCK // PANEL:
                rest = pl.ds((p + 1) * PANEL, BLOCK - (p + 1) * PANEL)
                fresh = split(fresh)
                old = z[m, rest, :]
                along = dot3(split(old), fresh, NT)
                z[m, rest, :] = old - dot3(split(along), fresh)


def step_kernel(
    held, wanted, grads, first, second, left_gram, right_gram, left, right,
    update, new_left, new_right, z, a_high, a_low, work, worst_ref, temp,
):
    @pl.loop(0, SLOTS)
    def _(s):
        new_left[s] = left[s]
        new_right[s] = right[s]

        @pl.when(held[s] == 0)
        def _():
            update[s] = jnp.zeros((BLOCK, BLOCK), f32)

        @pl.when(held[s] != 0)
        def _():
            g = grads[:, s].reshape(BLOCK, BLOCK)
            r = split(right[s])
            turned = split(left[s].T)
            temp[...] = dot(turned[0], g) + dot(turned[1], g)
            for c in range(0, BLOCK, CHUNK):
                rows = pl.ds(c, CHUNK)
                rotated = dot3(split(temp[rows, :]), r)
                moment = 0.9 * first[s, rows, :] + 0.1 * rotated
                spread = 0.95 * second[s, rows, :] + 0.05 * rotated * rotated
                temp[rows, :] = moment / (jnp.sqrt(spread) + 1e-08)
            normed = split(temp[...])
            for c in range(0, BLOCK, CHUNK):
                rows = pl.ds(c, CHUNK)
                back = dot3(split(left[s, rows, :]), normed)
                update[s, rows, :] = dot3(split(back), r, NT)

    @pl.when((wanted[0] + wanted[1]) != 0)
    def _():
        @pl.loop(0, SLOTS)
        def _(s):
            g = grads[:, s].reshape(BLOCK, BLOCK)
            gt = g.T
            for side, gram in enumerate((left_gram, right_gram)):
                m = SLOTS * s + side
                for c in range(0, BLOCK, CHUNK):
                    rows = pl.ds(c, CHUNK)
                    pieces = (g[c : c + CHUNK], g, NT) if side == 0 else (gt[c : c + CHUNK], g, NN)
                    high, low = split(0.95 * gram[s, rows, :] + 0.05 * dot(*pieces))
                    a_high[m, rows, :] = high
                    a_low[m, rows, :] = low

        def sweep(carry):
            phase, limit = carry

            @pl.when(phase < 2)
            def _():
                @pl.loop(0, SLOTS)
                def _(s):
                    z[SLOTS * s] = left[s].T
                    z[SLOTS * s + 1] = right[s].T

            worst_ref[...] = jnp.zeros((1, 128), f32)

            @pl.loop(0, MATS)
            def _(m):
                @pl.when(wanted[m // SLOTS] != 0)
                def _():
                    @pl.loop(0, jnp.where(phase == 0, 2, 1))
                    def _(_):
                        for c in range(0, BLOCK, CHUNK):
                            rows = pl.ds(c, CHUNK)
                            z[m, rows, :] = unit_rows(dot3(split(z[m, rows, :]), (a_high[m], a_low[m])))

            orthonormal_rows(z, work, worst_ref)
            slot = lax.broadcasted_iota(jnp.int32, (1, 128), 1) // (128 // SLOTS)
            counts = (slot == 0) & (wanted[0] != 0) | (slot == 1) & (wanted[1] != 0)
            bad = jnp.max(jnp.where(counts, worst_ref[...], 0.0)) > 0.5
            return phase + 1, jnp.where((phase == 0) & bad, 3, limit)

        lax.while_loop(lambda carry: carry[0] < carry[1], sweep, (jnp.int32(0), jnp.int32(1)))

        @pl.loop(0, SLOTS)
        def _(s):
            @pl.when(wanted[s] != 0)
            def _():
                new_left[s] = z[SLOTS * s].T
                new_right[s] = z[SLOTS * s + 1].T


def pack_kernel(table, gradient, outbox):
    @pl.loop(0, outbox.shape[0])
    def _(k):
        start = pl.multiple_of(jnp.maximum(table[k], 0) * BLOCK, BLOCK)
        piece = gradient[:, pl.ds(start, BLOCK)]
        outbox[k] = jnp.where(table[k] >= 0, piece, jnp.zeros_like(piece))


def step(held, wanted, grads, first, second, left_gram, right_gram, left, right):
    vmem = pl.BlockSpec(memory_space=pltpu.VMEM)
    smem = pl.BlockSpec(memory_space=pltpu.SMEM)
    whole = jax.ShapeDtypeStruct((SLOTS, BLOCK, BLOCK), f32)
    return pl.pallas_call(
        step_kernel,
        out_shape=(whole, whole, whole),
        in_specs=[smem, smem] + [vmem] * 7,
        out_specs=(vmem, vmem, vmem),
        scratch_shapes=[
            pltpu.VMEM((MATS, BLOCK, BLOCK), f32),
            pltpu.VMEM((MATS, BLOCK, BLOCK), bf16),
            pltpu.VMEM((MATS, BLOCK, BLOCK), bf16),
            pltpu.VMEM((MATS, PANEL, PANEL), f32),
            pltpu.VMEM((1, 128), f32),
            pltpu.VMEM((BLOCK, BLOCK), f32),
        ],
        compiler_params=pltpu.CompilerParams(vmem_limit_bytes=56 * 1024 * 1024),
    )(held, wanted, grads, first, second, left_gram, right_gram, left, right)


def local(
    gradient, slot_block, refresh_target, first_moment, second_moment, left_gram, right_gram, left_basis, right_basis
):
    owners = lax.axis_size("dp")
    owner = lax.axis_index("dp")
    device = owner * lax.axis_size("tensor") + lax.axis_index("tensor")
    table = slot_block[0]
    slab = gradient.shape[2]
    vmem = pl.BlockSpec(memory_space=pltpu.VMEM)
    smem = pl.BlockSpec(memory_space=pltpu.SMEM)
    outbox = pl.pallas_call(
        pack_kernel,
        out_shape=jax.ShapeDtypeStruct((owners * SLOTS, slab, BLOCK), bf16),
        in_specs=[smem, vmem],
        out_specs=vmem,
    )(table, gradient[0, 0])
    grads = lax.all_to_all(outbox.reshape(owners, SLOTS, slab, BLOCK), "dp", 0, 0, tiled=True)
    held = (lax.dynamic_slice_in_dim(table, owner * SLOTS, SLOTS) >= 0).astype(jnp.int32)
    wanted = (lax.dynamic_slice_in_dim(refresh_target, device * SLOTS, SLOTS) >= 0).astype(jnp.int32)
    outputs = step(
        held, wanted, grads, first_moment[0], second_moment[0], left_gram[0], right_gram[0], left_basis[0], right_basis[0]
    )
    return tuple(x[None] for x in outputs)


def solution(mesh):
    rows = P("tensor", "dp", None, None)
    return jax.shard_map(
        local,
        mesh=mesh,
        in_specs=(P("tensor", None, "dp", None), P("tensor", None), P(), rows, rows, rows, rows, rows, rows),
        out_specs=(rows, rows, rows),
        check_vma=False,
    )
```

```python
import functools

import jax
import jax.numpy as jnp
from jax import lax
from jax.experimental import pallas as pl
from jax.experimental.pallas import tpu as pltpu
from jax.sharding import PartitionSpec as P

BLOCK = 512
PANEL = 256
SUB = 128
LEAF = 32
SLOTS = 2
MATS = 2 * SLOTS
CHUNK = 256
WORST = 17.0

f32 = jnp.float32
bf16 = jnp.bfloat16

NN = (((1,), (0,)), ((), ()))
NT = (((1,), (1,)), ((), ()))
TN = (((0,), (0,)), ((), ()))


def split(x):
    high = x.astype(bf16)
    return high, (x - high.astype(f32)).astype(bf16)


def dot(a, b, dims=NN):
    return lax.dot_general(a, b, dims, preferred_element_type=f32)


def dot3(a, b, dims=NN):
    return dot(a[0], b[0], dims) + (dot(a[0], b[1], dims) + dot(a[1], b[0], dims))


def unit_rows(x):
    return x * lax.rsqrt(jnp.sum(x * x, axis=1, keepdims=True))


def leaf(tiles):
    lane = lax.broadcasted_iota(jnp.int32, (8, 128), 1)
    row = lax.broadcasted_iota(jnp.int32, (8, 128), 0)
    within = lane % LEAF
    base = lane - within
    worst = jnp.zeros((1, 128), f32)
    tiles = list(tiles)
    depth = LEAF // 8
    pick = lambda t, j: jnp.take_along_axis(tiles[t], base + j, axis=1)
    columns = [[pick(t, q) for t in range(depth)] for q in range(8)]
    for t0 in range(depth):
        ahead = [[pick(t, 8 * t0 + 8 + q) for t in range(t0 + 1, depth)] for q in range(8)] if t0 + 1 < depth else []
        for q in range(8):
            inverse = lax.rsqrt(columns[q][0][q : q + 1, :])
            worst = jnp.maximum(worst, jnp.where(inverse < WORST, 0.0, 1.0))
            factors = [column * inverse for column in columns[q]]
            factors[0] = jnp.where(row > q, factors[0], 0.0)
            for r in range(q + 1, 8):
                across = factors[0][r : r + 1, :]
                columns[r] = [column - factor * across for column, factor in zip(columns[r], factors)]
            here = within[:1] == 8 * t0 + q
            scaled = (tiles[t0][q : q + 1, :] + jnp.where(here, 1.0, 0.0)) * inverse
            for t in range(t0, depth):
                tiles[t] = tiles[t] - factors[t - t0] * scaled
            tiles[t0] = jnp.where(row == q, jnp.where(here, inverse, scaled), tiles[t0])
            for r in range(8 if ahead else 0):
                across = factors[1][r : r + 1, :]
                ahead[r] = [column - factor * across for column, factor in zip(ahead[r], factors[1:])]
        columns = ahead
    for t in range(LEAF // 8):
        tiles[t] = jnp.where(within <= row + 8 * t, tiles[t], 0.0)
    return tiles, worst


def rotated(x, m):
    cut = SUB - m * LEAF
    return x if m == 0 else jnp.concatenate([x[cut:], x[:cut]], axis=0)


def factor(work, worst_ref, tasks):
    lane = lax.broadcasted_iota(jnp.int32, (SUB, SUB), 1)
    row = lax.broadcasted_iota(jnp.int32, (SUB, SUB), 0)
    group = lane // LEAF
    own = group == row // LEAF
    for b in range(SUB // LEAF):
        top = b * LEAF
        rows = slice(top, top + LEAF)
        stacked = jnp.concatenate([work[(g - b) % MATS, rows, :] for g in range(MATS)], axis=0)
        packed = stacked[:LEAF]
        for g in range(1, MATS):
            packed = jnp.where(group[:LEAF] == g, stacked[g * LEAF : (g + 1) * LEAF], packed)
        tiles, worst = leaf([packed[8 * t : 8 * t + 8] for t in range(LEAF // 8)])
        tasks[b]()
        worst_ref[...] = jnp.maximum(worst_ref[...], worst)
        inverse = jnp.where(own, jnp.concatenate(tiles * MATS, axis=0), 0.0)
        pair = split(inverse)
        band = jnp.where(own, inverse, dot3(pair, split(stacked)))
        height = SUB - top - LEAF
        if height:
            under = slice(top + LEAF, SUB)
            old = jnp.concatenate([work[m, under, :] for m in range(MATS)], axis=0)
            mine = jnp.concatenate([group[:height] == (b + m) % MATS for m in range(MATS)], axis=0)
            factors = jnp.where(mine, dot3(split(old), pair, NT), 0.0)
            fresh = jnp.where(mine, 0.0, old) - dot3(split(factors), split(band))
            for m in range(MATS):
                work[m, under, :] = fresh[m * height : (m + 1) * height]
        for g in range(MATS):
            work[(g - b) % MATS, rows, :] = band[g * LEAF : (g + 1) * LEAF]
    for m in range(MATS):
        column = (lane + (SUB - m * LEAF)) % SUB
        work[m] = jnp.where(column <= row, work[m], 0.0)


def orthonormal_rows(z, work, low, turned_high, turned_low, worst_ref, wanted, tasks):
    lane = lax.broadcasted_iota(jnp.int32, (SUB, SUB), 1)
    row = lax.broadcasted_iota(jnp.int32, (SUB, SUB), 0)

    def guarded(m, x):
        unit = jnp.where((lane + (SUB - m * LEAF)) % SUB == row, 1.0, 0.0)
        return jnp.where(wanted[m // SLOTS] != 0, x, unit)

    for p in range(BLOCK // PANEL):
        here = slice(p * PANEL, (p + 1) * PANEL)
        for m in range(MATS):
            part = split(z[m, here, :])
            turned = tuple(jnp.concatenate([rotated(x[:SUB], m), rotated(x[SUB:], m)], axis=0) for x in part)
            turned_high[m] = turned[0]
            turned_low[m] = turned[1]
            product = dot3(part, turned, NT)
            work[m] = guarded(m, product[:SUB, :SUB])
            low[m] = product[SUB:, :SUB]
            z[m, PANEL * p + SUB : PANEL * (p + 1), :SUB] = product[SUB:, SUB:]
        factor(work, worst_ref, tasks[8 * p : 8 * p + 4])
        for m in range(MATS):
            inverse = split(work[m])
            across = split(dot3(split(low[m]), inverse, NT))
            gram_m = z[m, PANEL * p + SUB : PANEL * (p + 1), :SUB]
            low[m] = dot3(across, inverse)
            z[m, PANEL * p : PANEL * p + SUB, :SUB] = work[m]
            work[m] = guarded(m, gram_m - dot3(across, tuple(rotated(x, m) for x in across), NT))
        factor(work, worst_ref, tasks[8 * p + 4 : 8 * p + 8])
        for m in range(MATS):
            lower = split(work[m])
            cross = dot3(lower, tuple(rotated(x, m) for x in split(low[m])))
            upper = z[m, PANEL * p : PANEL * p + SUB, :SUB]
            whole = jnp.concatenate(
                [
                    jnp.concatenate([upper, jnp.zeros((SUB, SUB), f32)], axis=1),
                    jnp.concatenate([-cross, work[m]], axis=1),
                ],
                axis=0,
            )
            fresh = dot3(split(whole), (turned_high[m], turned_low[m]))
            z[m, here, :] = fresh
            if p + 1 < BLOCK // PANEL:
                rest = slice((p + 1) * PANEL, BLOCK)
                fresh = split(fresh)
                old = z[m, rest, :]
                along = dot3(split(old), fresh, NT)
                z[m, rest, :] = old - dot3(split(along), fresh)


def step_kernel(
    held, wanted, grads, first_in, second_in, left_gram_in, right_gram_in, left_in, right_in,
    update_out, new_left, new_right,
    g, first, second, left_gram, right_gram, left, right, update, left_high, left_low, temp,
    z, a_high, a_low, work, low, turned_high, turned_low, worst_ref, in_sems, out_sems,
):
    grams = (left_gram, right_gram)
    halves = [slice(c, c + CHUNK) for c in range(0, BLOCK, CHUNK)]
    g_copies = [pltpu.make_async_copy(grads.at[:, s], g.at[s], in_sems.at[s]) for s in range(SLOTS)]
    left_copy, right_copy, left_gram_copy, right_gram_copy, first_copy, second_copy = [
        pltpu.make_async_copy(source, target, in_sems.at[SLOTS + i])
        for i, (source, target) in enumerate(
            (
                (left_in, left),
                (right_in, right),
                (left_gram_in, left_gram),
                (right_gram_in, right_gram),
                (first_in, first),
                (second_in, second),
            )
        )
    ]
    left_copy.start()
    right_copy.start()
    for copy in g_copies:
        copy.start()
    left_gram_copy.start()
    right_gram_copy.start()
    first_copy.start()
    second_copy.start()

    def g_block(s):
        return g[s].reshape(BLOCK, BLOCK)

    def first_product(s, rows):
        temp[s, rows, :] = dot(left_high[s, rows, :], g_block(s)) + dot(left_low[s, rows, :], g_block(s))

    def moments(s, rows):
        rotated_rows = dot3(split(temp[s, rows, :]), split(right[s]))
        moment = 0.9 * first[s, rows, :] + 0.1 * rotated_rows
        spread = 0.95 * second[s, rows, :] + 0.05 * rotated_rows * rotated_rows
        temp[s, rows, :] = moment / (jnp.sqrt(spread) + 1e-08)

    def back(s, rows):
        update[s, rows, :] = dot3(split(left[s, rows, :]), split(temp[s]))

    def finish(s, rows):
        result = dot3(split(update[s, rows, :]), split(right[s]), NT)
        update[s, rows, :] = jnp.where(held[s] != 0, result, 0.0)

    refresh = (wanted[0] + wanted[1]) != 0
    left_copy.wait()
    right_copy.wait()

    @pl.when((held[0] + held[1]) != 0)
    def _():
        for s in range(SLOTS):
            high, low_part = split(left[s].T)
            left_high[s] = high
            left_low[s] = low_part

    for copy in g_copies:
        copy.wait()
    left_gram_copy.wait()
    right_gram_copy.wait()
    first_copy.wait()
    second_copy.wait()

    @pl.when(jnp.logical_not(refresh))
    def _():
        @pl.loop(0, SLOTS)
        def _(s):
            @pl.when(held[s] == 0)
            def _():
                update[s] = jnp.zeros((BLOCK, BLOCK), f32)

            @pl.when(held[s] != 0)
            def _():
                for stage in (first_product, moments, back, finish):
                    for rows in halves:
                        stage(s, rows)

    @pl.when(refresh)
    def _():
        @pl.loop(0, SLOTS)
        def _(s):
            gs = g_block(s)
            gt = gs.T
            for side in range(2):
                m = SLOTS * s + side
                for rows in halves:
                    pieces = (gs[rows], gs, NT) if side == 0 else (gt[rows], gs, NN)
                    high, low_part = split(0.95 * grams[side][s, rows, :] + 0.05 * dot(*pieces))
                    a_high[m, rows, :] = high
                    a_low[m, rows, :] = low_part

        def turn_back(m, columns):
            grams[m % 2][m // 2, :, columns] = z[m, columns, :].T

        tasks = []
        for stage in (first_product, moments, back, finish):
            for s in range(SLOTS):
                for rows in halves:
                    tasks.append(functools.partial(stage, s, rows))
        for m in range(MATS):
            tasks[8 + 2 * m] = functools.partial(
                lambda m, task: (task(), turn_back(m, slice(0, PANEL))), m, tasks[8 + 2 * m]
            )

        def sweep(carry):
            phase, limit = carry

            @pl.when(phase < 2)
            def _():
                @pl.loop(0, SLOTS)
                def _(s):
                    z[SLOTS * s] = left[s].T
                    z[SLOTS * s + 1] = right[s].T

            worst_ref[...] = jnp.zeros((1, 128), f32)

            @pl.loop(0, MATS)
            def _(m):
                @pl.when(wanted[m // SLOTS] != 0)
                def _():
                    @pl.loop(0, jnp.where(phase == 0, 2, 1))
                    def _(_):
                        for rows in halves:
                            z[m, rows, :] = unit_rows(dot3(split(z[m, rows, :]), (a_high[m], a_low[m])))

            orthonormal_rows(z, work, low, turned_high, turned_low, worst_ref, wanted, tasks)
            bad = jnp.max(worst_ref[...]) > 0.5
            return phase + 1, jnp.where((phase == 0) & bad, 3, limit)

        lax.while_loop(lambda carry: carry[0] < carry[1], sweep, (jnp.int32(0), jnp.int32(1)))

    update_copy = pltpu.make_async_copy(update, update_out, out_sems.at[0])
    update_copy.start()
    for m in range(MATS):
        s, side = divmod(m, 2)
        target = (new_left, new_right)[side].at[s]
        semaphore = out_sems.at[1 + m]

        @pl.when(wanted[s] != 0)
        def _():
            grams[side][s, :, PANEL:] = z[m, PANEL:, :].T
            pltpu.make_async_copy(grams[side].at[s], target, semaphore).start()

        @pl.when(wanted[s] == 0)
        def _():
            pltpu.make_async_copy((left, right)[side].at[s], target, semaphore).start()

    update_copy.wait()
    for m in range(MATS):
        s, side = divmod(m, 2)
        pltpu.make_async_copy(grams[side].at[s], (new_left, new_right)[side].at[s], out_sems.at[1 + m]).wait()


def pack_kernel(table, gradient, outbox):
    @pl.loop(0, outbox.shape[0])
    def _(k):
        start = pl.multiple_of(jnp.maximum(table[k], 0) * BLOCK, BLOCK)
        piece = gradient[:, pl.ds(start, BLOCK)]
        outbox[k] = jnp.where(table[k] >= 0, piece, jnp.zeros_like(piece))


def step(held, wanted, grads, first, second, left_gram, right_gram, left, right):
    anywhere = pl.BlockSpec(memory_space=pl.ANY)
    smem = pl.BlockSpec(memory_space=pltpu.SMEM)
    whole = jax.ShapeDtypeStruct((SLOTS, BLOCK, BLOCK), f32)
    return pl.pallas_call(
        step_kernel,
        out_shape=(whole, whole, whole),
        in_specs=[smem, smem] + [anywhere] * 7,
        out_specs=(anywhere, anywhere, anywhere),
        scratch_shapes=[pltpu.VMEM((SLOTS, *grads.shape[:1], *grads.shape[2:]), bf16)]
        + [pltpu.VMEM((SLOTS, BLOCK, BLOCK), f32)] * 7
        + [pltpu.VMEM((SLOTS, BLOCK, BLOCK), bf16)] * 2
        + [
            pltpu.VMEM((SLOTS, BLOCK, BLOCK), f32),
            pltpu.VMEM((MATS, BLOCK, BLOCK), f32),
            pltpu.VMEM((MATS, BLOCK, BLOCK), bf16),
            pltpu.VMEM((MATS, BLOCK, BLOCK), bf16),
            pltpu.VMEM((MATS, SUB, SUB), f32),
            pltpu.VMEM((MATS, SUB, SUB), f32),
            pltpu.VMEM((MATS, PANEL, BLOCK), bf16),
            pltpu.VMEM((MATS, PANEL, BLOCK), bf16),
            pltpu.VMEM((1, 128), f32),
            pltpu.SemaphoreType.DMA((SLOTS + 6,)),
            pltpu.SemaphoreType.DMA((1 + MATS,)),
        ],
        compiler_params=pltpu.CompilerParams(vmem_limit_bytes=48 * 1024 * 1024),
    )(held, wanted, grads, first, second, left_gram, right_gram, left, right)


def local(
    gradient, slot_block, refresh_target, first_moment, second_moment, left_gram, right_gram, left_basis, right_basis
):
    owners = lax.axis_size("dp")
    owner = lax.axis_index("dp")
    device = owner * lax.axis_size("tensor") + lax.axis_index("tensor")
    table = slot_block[0]
    slab = gradient.shape[2]
    vmem = pl.BlockSpec(memory_space=pltpu.VMEM)
    smem = pl.BlockSpec(memory_space=pltpu.SMEM)
    outbox = pl.pallas_call(
        pack_kernel,
        out_shape=jax.ShapeDtypeStruct((owners * SLOTS, slab, BLOCK), bf16),
        in_specs=[smem, vmem],
        out_specs=vmem,
    )(table, gradient[0, 0])
    grads = lax.all_to_all(outbox.reshape(owners, SLOTS, slab, BLOCK), "dp", 0, 0, tiled=True)
    held = (lax.dynamic_slice_in_dim(table, owner * SLOTS, SLOTS) >= 0).astype(jnp.int32)
    wanted = (lax.dynamic_slice_in_dim(refresh_target, device * SLOTS, SLOTS) >= 0).astype(jnp.int32)
    outputs = step(
        held, wanted, grads, first_moment[0], second_moment[0], left_gram[0], right_gram[0], left_basis[0], right_basis[0]
    )
    return tuple(x[None] for x in outputs)


def solution(mesh):
    rows = P("tensor", "dp", None, None)
    return jax.shard_map(
        local,
        mesh=mesh,
        in_specs=(P("tensor", None, "dp", None), P("tensor", None), P(), rows, rows, rows, rows, rows, rows),
        out_specs=(rows, rows, rows),
        check_vma=False,
    )
```

```python
import functools

import jax
import jax.numpy as jnp
from jax import lax
from jax.experimental import pallas as pl
from jax.experimental.pallas import tpu as pltpu
from jax.sharding import PartitionSpec as P

BLOCK = 512
SUB = 128
LEAF = 32
SLOTS = 2
MATS = 2 * SLOTS
CHUNK = 256
WORST = 10.0
LEAF_WEIGHTS = [2, 2, 2, 2, 2, 2]

f32 = jnp.float32
bf16 = jnp.bfloat16

NN = (((1,), (0,)), ((), ()))
NT = (((1,), (1,)), ((), ()))
TN = (((0,), (0,)), ((), ()))


def split(x):
    high = x.astype(bf16)
    return high, (x - high.astype(f32)).astype(bf16)


def dot(a, b, dims=NN):
    return lax.dot_general(a, b, dims, preferred_element_type=f32)


def dot3(a, b, dims=NN):
    return dot(a[0], b[0], dims) + (dot(a[0], b[1], dims) + dot(a[1], b[0], dims))


def dot3_tile(a, b, dims=NN):
    zeros = jnp.zeros((SUB, SUB), bf16)
    if dims == NN:
        top, bottom = (b[0], b[1]), (b[0], zeros)
    else:
        top, bottom = (b[0], b[0]), (b[1], zeros)
    operand = jnp.concatenate([jnp.concatenate(top, axis=1), jnp.concatenate(bottom, axis=1)], axis=0)
    result = dot(jnp.concatenate(a, axis=1), operand, dims)
    return result[:, :SUB] + result[:, SUB:]


def dot3_deep(a, b):
    return dot(jnp.concatenate(a, axis=1), jnp.concatenate([b[0], b[0]], axis=0)) + dot(a[0], b[1])


def dot3_narrow(a, b):
    result = dot(a[0], jnp.concatenate(b, axis=0), NT)
    return result[:, :SUB] + (result[:, SUB:] + dot(a[1], b[0], NT))


def unit_rows(x):
    return x * lax.rsqrt(jnp.sum(x * x, axis=1, keepdims=True))


def leaf(tiles, hooks):
    lane = lax.broadcasted_iota(jnp.int32, (8, 128), 1)
    row = lax.broadcasted_iota(jnp.int32, (8, 128), 0)
    within = lane % LEAF
    base = lane - within
    worst = jnp.zeros((1, 128), f32)
    tiles = list(tiles)
    depth = LEAF // 8
    pick = lambda t, j: jnp.take_along_axis(tiles[t], base + j, axis=1)
    columns = [[pick(t, q) for t in range(depth)] for q in range(8)]
    for t0 in range(depth):
        ahead = [[pick(t, 8 * t0 + 8 + q) for t in range(t0 + 1, depth)] for q in range(8)] if t0 + 1 < depth else []
        for q in range(8):
            inverse = lax.rsqrt(columns[q][0][q : q + 1, :])
            worst = jnp.maximum(worst, jnp.where(inverse < WORST, 0.0, 1.0))
            factors = [column * inverse for column in columns[q]]
            factors[0] = jnp.where(row > q, factors[0], 0.0)
            for r in range(q + 1, 8):
                across = factors[0][r : r + 1, :]
                columns[r] = [column - factor * across for column, factor in zip(columns[r], factors)]
            here = within[:1] == 8 * t0 + q
            scaled = (tiles[t0][q : q + 1, :] + jnp.where(here, 1.0, 0.0)) * inverse
            for t in range(t0, depth):
                tiles[t] = tiles[t] - factors[t - t0] * scaled
            tiles[t0] = jnp.where(row == q, jnp.where(here, inverse, scaled), tiles[t0])
            for r in range(8 if ahead else 0):
                across = factors[1][r : r + 1, :]
                ahead[r] = [column - factor * across for column, factor in zip(ahead[r], factors[1:])]
        columns = ahead
        hooks[t0]()
    for t in range(LEAF // 8):
        tiles[t] = jnp.where(within <= row + 8 * t, tiles[t], 0.0)
    return tiles, worst


def rotated(x, m):
    cut = SUB - m * LEAF
    return x if m == 0 else jnp.concatenate([x[cut:], x[:cut]], axis=0)


def factor(work, worst_ref, tasks):
    lane = lax.broadcasted_iota(jnp.int32, (SUB, SUB), 1)
    row = lax.broadcasted_iota(jnp.int32, (SUB, SUB), 0)
    group = lane // LEAF
    own = group == row // LEAF
    steps = SUB // LEAF
    current = [work[m, :LEAF, :] for m in range(MATS)]
    for b in range(steps):
        rows = slice(b * LEAF, (b + 1) * LEAF)
        stacked = jnp.concatenate([current[(g - b) % MATS] for g in range(MATS)], axis=0)
        packed = stacked[:LEAF]
        for g in range(1, MATS):
            packed = jnp.where(group[:LEAF] == g, stacked[g * LEAF : (g + 1) * LEAF], packed)
        tiles, worst = leaf([packed[8 * t : 8 * t + 8] for t in range(LEAF // 8)], tasks[6 * b : 6 * b + 4])
        worst_ref[...] = jnp.maximum(worst_ref[...], worst)
        inverse = jnp.where(own, jnp.concatenate(tiles * MATS, axis=0), 0.0)
        pair = split(inverse)

        height = SUB - (b + 2) * LEAF
        if b + 1 < steps:
            following = slice((b + 1) * LEAF, (b + 2) * LEAF)
            pieces = [(m, following, LEAF) for m in range(MATS)]
            if height:
                pieces += [(m, slice((b + 2) * LEAF, SUB), height) for m in range(MATS)]
            old = jnp.concatenate([work[m, under, :] for m, under, _ in pieces], axis=0)
            mine = jnp.concatenate([group[:size] == (b + m) % MATS for m, _, size in pieces], axis=0)
            factors = jnp.where(mine, dot3_tile(split(old), pair, NT), 0.0)
        band = jnp.where(own, inverse, dot3_tile(pair, split(stacked)))
        tasks[6 * b + 4]()
        if b + 1 < steps:
            fresh = jnp.where(mine, 0.0, old) - dot3_tile(split(factors), split(band))
            current = [fresh[m * LEAF : (m + 1) * LEAF] for m in range(MATS)]
            for m in range(MATS if height else 0):
                start = MATS * LEAF + m * height
                work[m, (b + 2) * LEAF :, :] = fresh[start : start + height]
        tasks[6 * b + 5]()
        for g in range(MATS):
            work[(g - b) % MATS, rows, :] = band[g * LEAF : (g + 1) * LEAF]
    for m in range(MATS):
        column = (lane + (SUB - m * LEAF)) % SUB
        work[m] = jnp.where(column <= row, work[m], 0.0)


def spread_out(tasks, weights):
    total = sum(cost for cost, _ in tasks)
    edges = [total * sum(weights[: i + 1]) / sum(weights) for i in range(len(weights))]
    shares = [[] for _ in weights]
    done = 0.0
    at = 0
    for cost, call in tasks:
        while at + 1 < len(weights) and done + cost / 2 > edges[at]:
            at += 1
        shares[at].append(call)
        done += cost

    def run(calls):
        for call in calls:
            call()

    return [functools.partial(run, calls) for calls in shares]


def prepare_kernel(
    left_in, right_in, left_gram_in, right_gram_in, first_in, second_in,
    turned, left, right, right_high, right_low, left_gram, right_gram, first, second, sems,
):
    copies = [
        pltpu.make_async_copy(source, target, sems.at[i])
        for i, (source, target) in enumerate(
            (
                (left_in, left),
                (right_in, right),
                (left_gram_in, left_gram),
                (right_gram_in, right_gram),
                (first_in, first),
                (second_in, second),
            )
        )
    ]
    for copy in copies:
        copy.start()
    copies[0].wait()
    for s in range(SLOTS):
        turned[2 * s] = left[s].T
    copies[1].wait()
    for s in range(SLOTS):
        turned[2 * s + 1] = right[s].T
        right_high[s], right_low[s] = split(right[s])
    for copy in copies[2:]:
        copy.wait()


def step_kernel(
    held, wanted, grads, turned, left, right, right_high, right_low, left_gram, right_gram, first, second,
    update_out, new_left, new_right,
    g, update, temp, z, a_high, a_low, work, near, square, fresh, worst_ref, in_sems, out_sems,
):
    halves = [slice(c, c + CHUNK) for c in range(0, BLOCK, CHUNK)]
    blocks = [slice(c, c + SUB) for c in range(0, BLOCK, SUB)]
    g_copies = [pltpu.make_async_copy(grads.at[:, s], g.at[s], in_sems.at[s]) for s in range(SLOTS)]
    for copy in g_copies:
        copy.start()
    for copy in g_copies:
        copy.wait()

    def g_block(s):
        return g[s].reshape(BLOCK, BLOCK)

    def right_pair(s):
        return right_high[s], right_low[s]

    def first_product(s, rows):
        high, low = split(turned[2 * s, rows, :])
        temp[s, rows, :] = dot(high, g_block(s)) + dot(low, g_block(s))

    def moments(s, rows):
        rotated_rows = dot3(split(temp[s, rows, :]), right_pair(s))
        moment = 0.9 * first[s, rows, :] + 0.1 * rotated_rows
        spread = 0.95 * second[s, rows, :] + 0.05 * rotated_rows * rotated_rows
        temp[s, rows, :] = moment / (jnp.sqrt(spread) + 1e-08)

    def back(s, rows):
        update[s, rows, :] = dot3(split(left[s, rows, :]), split(temp[s]))

    def finish(s, rows):
        result = dot3(split(update[s, rows, :]), right_pair(s), NT)
        update[s, rows, :] = jnp.where(held[s] != 0, result, 0.0)

    refresh = (wanted[0] + wanted[1]) != 0

    @pl.when(jnp.logical_not(refresh))
    def _():
        @pl.loop(0, SLOTS)
        def _(s):
            @pl.when(held[s] == 0)
            def _():
                update[s] = jnp.zeros((BLOCK, BLOCK), f32)

            @pl.when(held[s] != 0)
            def _():
                for stage in (first_product, moments, back, finish):
                    for rows in halves:
                        stage(s, rows)

    @pl.when(refresh)
    def _():
        for s in range(SLOTS):
            gs = g_block(s)
            gt = gs.T
            for side in range(2):
                m = SLOTS * s + side
                for rows in halves:
                    pieces = (gs[rows], gs, NT) if side == 0 else (gt[rows], gs, NN)
                    past = (left_gram, right_gram)[side][s, rows, :]
                    a_high[m, rows, :], a_low[m, rows, :] = split(0.95 * past + 0.05 * dot(*pieces))

        def sweep(carry):
            phase, limit = carry
            worst_ref[...] = jnp.zeros((1, 128), f32)
            lane = lax.broadcasted_iota(jnp.int32, (SUB, SUB), 1)
            row = lax.broadcasted_iota(jnp.int32, (SUB, SUB), 0)

            def power(m, j):
                rows = blocks[j]
                source = jnp.where(phase == 2, z[m, rows, :], turned[m, rows, :])
                z[m, rows, :] = unit_rows(dot3(split(source), (a_high[m], a_low[m])))

            def again(m, j):
                rows = blocks[j]
                once = z[m, rows, :]
                z[m, rows, :] = jnp.where(phase == 0, unit_rows(dot3(split(once), (a_high[m], a_low[m]))), once)

            def products(m, j):
                part = split(z[m, blocks[j], :])
                other = [tuple(rotated(x, m) for x in part)]
                if j:
                    other.append(tuple(rotated(x, m) for x in split(z[m, blocks[j - 1], :])))
                result = dot3(part, tuple(jnp.concatenate(x, axis=0) for x in zip(*other)), NT) if j else dot3_narrow(part, other[0])
                square[m] = result[:, :SUB]
                if j:
                    near[m] = result[:, SUB:]

            def couple(m, j):
                value = dot3_tile(split(near[m]), split(inverses[j - 1][m]), NT)
                near[m] = value
                value = split(value)
                square[m] -= dot3_tile(value, tuple(rotated(x, m) for x in value), NT)

            def project(m, j):
                z[m, blocks[j], :] -= dot3_deep(split(near[m]), split(z[m, blocks[j - 1], :]))

            def align(m, j, count):
                fixed = split(z[m, : count * SUB, :])
                part = split(z[m, blocks[j], :])
                if count == 1:
                    z[m, blocks[j], :] -= dot3_deep(split(dot3_narrow(part, fixed)), fixed)
                else:
                    z[m, blocks[j], :] -= dot3(split(dot3(part, fixed, NT)), fixed)

            def scale(m, j):
                part = tuple(rotated(x, m) for x in split(z[m, blocks[j], :]))
                z[m, blocks[j], :] = dot3_deep(split(inverses[j][m]), part)

            def turn_back(m, columns):
                fresh[m, :, columns] = z[m, columns, :].T

            def guarded(m, x):
                unit = jnp.where((lane + (SUB - m * LEAF)) % SUB == row, 1.0, 0.0)
                return jnp.where(wanted[m // SLOTS] != 0, x, unit)

            def every(cost, task, *more):
                return [(cost, functools.partial(task, m, *more)) for m in range(MATS)]

            def step_tasks(cost, stage):
                return [(cost, functools.partial(stage, s, rows)) for s in range(SLOTS) for rows in blocks]

            inverses = [None] * len(blocks)
            firsts, middles, backs, ends = (
                step_tasks(cost, stage) for cost, stage in ((2, first_product), (3, moments), (3, back), (3, finish))
            )
            windows = [
                every(3, power, 1) + every(3, again, 1) + every(1, products, 1) + every(3, power, 2) + every(3, again, 2) + firsts,
                every(1, scale, 0) + every(1, project, 1) + every(2, align, 2, 1) + every(1, products, 2)
                + every(3, power, 3) + every(3, again, 3) + middles[:4],
                every(1, scale, 1) + every(1, project, 2) + every(2, align, 3, 2) + every(1, products, 3) + middles[4:] + backs[:4],
                every(1, scale, 2) + every(1, project, 3) + backs[4:] + ends + every(2, turn_back, slice(0, 3 * SUB)),
            ]
            weights = LEAF_WEIGHTS * (SUB // LEAF)
            for m in range(MATS):
                power(m, 0)
            for m in range(MATS):
                again(m, 0)
            for m in range(MATS):
                products(m, 0)
            for j in range(len(blocks)):
                for m in range(MATS):
                    if j:
                        couple(m, j)
                    work[m] = guarded(m, square[m])
                factor(work, worst_ref, spread_out(windows[j], weights))
                inverses[j] = [work[m] for m in range(MATS)]
            for m in range(MATS):
                scale(m, len(blocks) - 1)
            bad = jnp.max(worst_ref[...]) > 0.5
            return phase + 1, jnp.where((phase == 0) & bad, 3, limit)

        lax.while_loop(lambda carry: carry[0] < carry[1], sweep, (jnp.int32(0), jnp.int32(1)))

    update_copy = pltpu.make_async_copy(update, update_out, out_sems.at[0])
    update_copy.start()
    for m in range(MATS):
        s, side = divmod(m, 2)
        target = (new_left, new_right)[side].at[s]
        semaphore = out_sems.at[1 + m]

        @pl.when(wanted[s] != 0)
        def _():
            fresh[m, :, blocks[-1]] = z[m, blocks[-1], :].T
            pltpu.make_async_copy(fresh.at[m], target, semaphore).start()

        @pl.when(wanted[s] == 0)
        def _():
            pltpu.make_async_copy((left, right)[side].at[s], target, semaphore).start()

    update_copy.wait()
    for m in range(MATS):
        s, side = divmod(m, 2)
        pltpu.make_async_copy(fresh.at[m], (new_left, new_right)[side].at[s], out_sems.at[1 + m]).wait()


def pack_kernel(table, gradient, outbox):
    @pl.loop(0, outbox.shape[0])
    def _(k):
        start = pl.multiple_of(jnp.maximum(table[k], 0) * BLOCK, BLOCK)
        piece = gradient[:, pl.ds(start, BLOCK)]
        outbox[k] = jnp.where(table[k] >= 0, piece, jnp.zeros_like(piece))


def prepare(left, right, left_gram, right_gram, first, second):
    anywhere = pl.BlockSpec(memory_space=pl.ANY)
    vmem = pl.BlockSpec(memory_space=pltpu.VMEM)
    whole = pltpu.VMEM((SLOTS, BLOCK, BLOCK), f32)
    short = pltpu.VMEM((SLOTS, BLOCK, BLOCK), bf16)
    inputs = (left, right, left_gram, right_gram, first, second)
    return pl.pallas_call(
        prepare_kernel,
        out_shape=(pltpu.VMEM((MATS, BLOCK, BLOCK), f32), whole, whole, short, short, whole, whole, whole, whole),
        in_specs=[anywhere] * len(inputs),
        out_specs=(vmem,) * 9,
        scratch_shapes=[pltpu.SemaphoreType.DMA((len(inputs),))],
        compiler_params=pltpu.CompilerParams(vmem_limit_bytes=4 * 1024 * 1024),
        cost_estimate=pl.CostEstimate(flops=8_000_000, bytes_accessed=32 * 1024 * 1024, transcendentals=0),
    )(*(pltpu.with_memory_space_constraint(x, pltpu.HBM) for x in inputs))


def step(held, wanted, grads, prepared):
    anywhere = pl.BlockSpec(memory_space=pl.ANY)
    vmem = pl.BlockSpec(memory_space=pltpu.VMEM)
    smem = pl.BlockSpec(memory_space=pltpu.SMEM)
    whole = jax.ShapeDtypeStruct((SLOTS, BLOCK, BLOCK), f32)
    return pl.pallas_call(
        step_kernel,
        out_shape=(whole, whole, whole),
        in_specs=[smem, smem, anywhere] + [vmem] * len(prepared),
        out_specs=(anywhere, anywhere, anywhere),
        scratch_shapes=[
            pltpu.VMEM((SLOTS, *grads.shape[:1], *grads.shape[2:]), bf16),
            pltpu.VMEM((SLOTS, BLOCK, BLOCK), f32),
            pltpu.VMEM((SLOTS, BLOCK, BLOCK), f32),
            pltpu.VMEM((MATS, BLOCK, BLOCK), f32),
            pltpu.VMEM((MATS, BLOCK, BLOCK), bf16),
            pltpu.VMEM((MATS, BLOCK, BLOCK), bf16),
            pltpu.VMEM((MATS, SUB, SUB), f32),
            pltpu.VMEM((MATS, SUB, SUB), f32),
            pltpu.VMEM((MATS, SUB, SUB), f32),
            pltpu.VMEM((MATS, BLOCK, BLOCK), f32),
            pltpu.VMEM((1, 128), f32),
            pltpu.SemaphoreType.DMA((SLOTS,)),
            pltpu.SemaphoreType.DMA((1 + MATS,)),
        ],
        compiler_params=pltpu.CompilerParams(vmem_limit_bytes=36 * 1024 * 1024),
    )(
        held,
        wanted,
        pltpu.with_memory_space_constraint(grads, pltpu.HBM),
        *(pltpu.with_memory_space_constraint(x, pltpu.VMEM) for x in prepared),
    )


def local(
    gradient, slot_block, refresh_target, first_moment, second_moment, left_gram, right_gram, left_basis, right_basis
):
    owners = lax.axis_size("dp")
    owner = lax.axis_index("dp")
    device = owner * lax.axis_size("tensor") + lax.axis_index("tensor")
    table = slot_block[0]
    slab = gradient.shape[2]
    vmem = pl.BlockSpec(memory_space=pltpu.VMEM)
    smem = pl.BlockSpec(memory_space=pltpu.SMEM)
    outbox = pl.pallas_call(
        pack_kernel,
        out_shape=jax.ShapeDtypeStruct((owners * SLOTS, slab, BLOCK), bf16),
        in_specs=[smem, vmem],
        out_specs=vmem,
    )(table, gradient[0, 0])
    grads = lax.all_to_all(outbox.reshape(owners, SLOTS, slab, BLOCK), "dp", 0, 0, tiled=True)
    held = (lax.dynamic_slice_in_dim(table, owner * SLOTS, SLOTS) >= 0).astype(jnp.int32)
    wanted = (lax.dynamic_slice_in_dim(refresh_target, device * SLOTS, SLOTS) >= 0).astype(jnp.int32)
    prepared = prepare(left_basis[0], right_basis[0], left_gram[0], right_gram[0], first_moment[0], second_moment[0])
    outputs = step(held, wanted, grads, prepared)
    return tuple(x[None] for x in outputs)


def solution(mesh):
    rows = P("tensor", "dp", None, None)
    return jax.shard_map(
        local,
        mesh=mesh,
        in_specs=(P("tensor", None, "dp", None), P("tensor", None), P(), rows, rows, rows, rows, rows, rows),
        out_specs=(rows, rows, rows),
        check_vma=False,
    )
```

```python
import functools

import jax
import jax.numpy as jnp
from jax import lax
from jax.experimental import pallas as pl
from jax.experimental.pallas import tpu as pltpu
from jax.sharding import PartitionSpec as P

BLOCK = 512
SUB = 128
LEAF = 32
SLOTS = 2
MATS = 2 * SLOTS
CHUNK = 256
WORST = 10.0
LEAF_WEIGHTS = [2, 2, 2, 2, 2, 2]

f32 = jnp.float32
bf16 = jnp.bfloat16

NN = (((1,), (0,)), ((), ()))
NT = (((1,), (1,)), ((), ()))
TN = (((0,), (0,)), ((), ()))


def split(x):
    high = x.astype(bf16)
    return high, (x - high.astype(f32)).astype(bf16)


def dot(a, b, dims=NN):
    return lax.dot_general(a, b, dims, preferred_element_type=f32)


def dot3(a, b, dims=NN):
    return dot(a[0], b[0], dims) + (dot(a[0], b[1], dims) + dot(a[1], b[0], dims))


def dot3_tile(a, b, dims=NN):
    zeros = jnp.zeros((SUB, SUB), bf16)
    if dims == NN:
        top, bottom = (b[0], b[1]), (b[0], zeros)
    else:
        top, bottom = (b[0], b[0]), (b[1], zeros)
    operand = jnp.concatenate([jnp.concatenate(top, axis=1), jnp.concatenate(bottom, axis=1)], axis=0)
    result = dot(jnp.concatenate(a, axis=1), operand, dims)
    return result[:, :SUB] + result[:, SUB:]


def dot3_deep(a, b):
    return dot(jnp.concatenate(a, axis=1), jnp.concatenate([b[0], b[0]], axis=0)) + dot(a[0], b[1])


def dot3_narrow(a, b):
    result = dot(a[0], jnp.concatenate(b, axis=0), NT)
    return result[:, :SUB] + (result[:, SUB:] + dot(a[1], b[0], NT))


def unit_rows(x):
    return x * lax.rsqrt(jnp.sum(x * x, axis=1, keepdims=True))


def leaf(tiles, hooks):
    lane = lax.broadcasted_iota(jnp.int32, (8, 128), 1)
    row = lax.broadcasted_iota(jnp.int32, (8, 128), 0)
    within = lane % LEAF
    base = lane - within
    worst = jnp.zeros((1, 128), f32)
    tiles = list(tiles)
    depth = LEAF // 8
    pick = lambda t, j: jnp.take_along_axis(tiles[t], base + j, axis=1)
    columns = [[pick(t, q) for t in range(depth)] for q in range(8)]
    for t0 in range(depth):
        ahead = [[pick(t, 8 * t0 + 8 + q) for t in range(t0 + 1, depth)] for q in range(8)] if t0 + 1 < depth else []
        for q in range(8):
            inverse = lax.rsqrt(columns[q][0][q : q + 1, :])
            worst = jnp.maximum(worst, jnp.where(inverse < WORST, 0.0, 1.0))
            factors = [column * inverse for column in columns[q]]
            factors[0] = jnp.where(row > q, factors[0], 0.0)
            for r in range(q + 1, 8):
                across = factors[0][r : r + 1, :]
                columns[r] = [column - factor * across for column, factor in zip(columns[r], factors)]
            here = within[:1] == 8 * t0 + q
            scaled = (tiles[t0][q : q + 1, :] + jnp.where(here, 1.0, 0.0)) * inverse
            for t in range(t0, depth):
                tiles[t] = tiles[t] - factors[t - t0] * scaled
            tiles[t0] = jnp.where(row == q, jnp.where(here, inverse, scaled), tiles[t0])
            for r in range(8 if ahead else 0):
                across = factors[1][r : r + 1, :]
                ahead[r] = [column - factor * across for column, factor in zip(ahead[r], factors[1:])]
        columns = ahead
        hooks[t0]()
    for t in range(LEAF // 8):
        tiles[t] = jnp.where(within <= row + 8 * t, tiles[t], 0.0)
    return tiles, worst


def rotated(x, m):
    cut = SUB - m * LEAF
    return x if m == 0 else jnp.concatenate([x[cut:], x[:cut]], axis=0)


def factor(work, worst_ref, tasks):
    lane = lax.broadcasted_iota(jnp.int32, (SUB, SUB), 1)
    row = lax.broadcasted_iota(jnp.int32, (SUB, SUB), 0)
    group = lane // LEAF
    own = group == row // LEAF
    steps = SUB // LEAF
    current = [work[m, :LEAF, :] for m in range(MATS)]
    for b in range(steps):
        rows = slice(b * LEAF, (b + 1) * LEAF)
        stacked = jnp.concatenate([current[(g - b) % MATS] for g in range(MATS)], axis=0)
        packed = stacked[:LEAF]
        for g in range(1, MATS):
            packed = jnp.where(group[:LEAF] == g, stacked[g * LEAF : (g + 1) * LEAF], packed)
        tiles, worst = leaf([packed[8 * t : 8 * t + 8] for t in range(LEAF // 8)], tasks[6 * b : 6 * b + 4])
        worst_ref[...] = jnp.maximum(worst_ref[...], worst)
        inverse = jnp.where(own, jnp.concatenate(tiles * MATS, axis=0), 0.0)
        pair = split(inverse)

        height = SUB - (b + 2) * LEAF
        if b + 1 < steps:
            following = slice((b + 1) * LEAF, (b + 2) * LEAF)
            pieces = [(m, following, LEAF) for m in range(MATS)]
            if height:
                pieces += [(m, slice((b + 2) * LEAF, SUB), height) for m in range(MATS)]
            old = jnp.concatenate([work[m, under, :] for m, under, _ in pieces], axis=0)
            mine = jnp.concatenate([group[:size] == (b + m) % MATS for m, _, size in pieces], axis=0)
            factors = jnp.where(mine, dot3_tile(split(old), pair, NT), 0.0)
        band = jnp.where(own, inverse, dot3_tile(pair, split(stacked)))
        tasks[6 * b + 4]()
        if b + 1 < steps:
            fresh = jnp.where(mine, 0.0, old) - dot3_tile(split(factors), split(band))
            current = [fresh[m * LEAF : (m + 1) * LEAF] for m in range(MATS)]
            for m in range(MATS if height else 0):
                start = MATS * LEAF + m * height
                work[m, (b + 2) * LEAF :, :] = fresh[start : start + height]
        tasks[6 * b + 5]()
        for g in range(MATS):
            work[(g - b) % MATS, rows, :] = band[g * LEAF : (g + 1) * LEAF]
    for m in range(MATS):
        column = (lane + (SUB - m * LEAF)) % SUB
        work[m] = jnp.where(column <= row, work[m], 0.0)


def spread_out(tasks, weights):
    total = sum(cost for cost, _ in tasks)
    edges = [total * sum(weights[: i + 1]) / sum(weights) for i in range(len(weights))]
    shares = [[] for _ in weights]
    done = 0.0
    at = 0
    for cost, call in tasks:
        while at + 1 < len(weights) and done + cost / 2 > edges[at]:
            at += 1
        shares[at].append(call)
        done += cost

    def run(calls):
        for call in calls:
            call()

    return [functools.partial(run, calls) for calls in shares]


def prepare_kernel(left, right, turned, right_high, right_low):
    for s in range(SLOTS):
        turned[2 * s] = left[s].T
        turned[2 * s + 1] = right[s].T
        right_high[s], right_low[s] = split(right[s])


def step_kernel(
    held, wanted, grads, turned_in, left_in, right_high_in, right_low_in, left_gram_in, right_gram_in, first_in, second_in, right_in,
    update_out, new_left, new_right,
    g, turned, left, right_high, right_low, left_gram, right_gram, first, second,
    update, temp, z, a_high, a_low, work, near, square, fresh, worst_ref, in_sems, out_sems,
):
    halves = [slice(c, c + CHUNK) for c in range(0, BLOCK, CHUNK)]
    blocks = [slice(c, c + SUB) for c in range(0, BLOCK, SUB)]
    used = []

    def copy_in(source, target):
        used.append(pltpu.make_async_copy(source, target, in_sems.at[len(used)]))
        return used[-1]

    early = [
        [
            copy_in(grads.at[:, s], g.at[s]),
            copy_in(left_gram_in.at[s], left_gram.at[s]),
            copy_in(right_gram_in.at[s], right_gram.at[s]),
        ]
        for s in range(SLOTS)
    ]
    middle = copy_in(turned_in, turned)
    late = [
        copy_in(source, target)
        for source, target in (
            (right_high_in, right_high),
            (right_low_in, right_low),
            (first_in, first),
            (second_in, second),
            (left_in, left),
        )
    ]
    for copies in early:
        for copy in copies:
            copy.start()
    middle.start()
    for copy in early[0]:
        copy.wait()
    for copy in late:
        copy.start()

    for m in range(MATS):
        s, side = divmod(m, 2)

        @pl.when(wanted[s] == 0)
        def _():
            unchanged = (left_in, right_in)[side].at[s]
            pltpu.make_async_copy(unchanged, (new_left, new_right)[side].at[s], out_sems.at[1 + m]).start()

    def wait_late():
        for copy in late:
            copy.wait()

    def g_block(s):
        return g[s].reshape(BLOCK, BLOCK)

    def right_pair(s):
        return right_high[s], right_low[s]

    def first_product(s, rows):
        high, low = split(turned[2 * s, rows, :])
        temp[s, rows, :] = dot(high, g_block(s)) + dot(low, g_block(s))

    def moments(s, rows):
        rotated_rows = dot3(split(temp[s, rows, :]), right_pair(s))
        moment = 0.9 * first[s, rows, :] + 0.1 * rotated_rows
        spread = 0.95 * second[s, rows, :] + 0.05 * rotated_rows * rotated_rows
        temp[s, rows, :] = moment / (jnp.sqrt(spread) + 1e-08)

    def back(s, rows):
        update[s, rows, :] = dot3(split(left[s, rows, :]), split(temp[s]))

    def finish(s, rows):
        result = dot3(split(update[s, rows, :]), right_pair(s), NT)
        update[s, rows, :] = jnp.where(held[s] != 0, result, 0.0)

    refresh = (wanted[0] + wanted[1]) != 0

    @pl.when(jnp.logical_not(refresh))
    def _():
        for copy in early[1]:
            copy.wait()
        middle.wait()
        wait_late()

        @pl.loop(0, SLOTS)
        def _(s):
            @pl.when(held[s] == 0)
            def _():
                update[s] = jnp.zeros((BLOCK, BLOCK), f32)

            @pl.when(held[s] != 0)
            def _():
                for stage in (first_product, moments, back, finish):
                    for rows in halves:
                        stage(s, rows)

    @pl.when(refresh)
    def _():
        for s in range(SLOTS):
            if s:
                for copy in early[s]:
                    copy.wait()
            gs = g_block(s)
            gt = gs.T
            for side in range(2):
                m = SLOTS * s + side
                for rows in halves:
                    pieces = (gs[rows], gs, NT) if side == 0 else (gt[rows], gs, NN)
                    past = (left_gram, right_gram)[side][s, rows, :]
                    a_high[m, rows, :], a_low[m, rows, :] = split(0.95 * past + 0.05 * dot(*pieces))

        middle.wait()

        def sweep(carry):
            phase, limit = carry
            worst_ref[...] = jnp.zeros((1, 128), f32)
            lane = lax.broadcasted_iota(jnp.int32, (SUB, SUB), 1)
            row = lax.broadcasted_iota(jnp.int32, (SUB, SUB), 0)

            def power(m, j):
                rows = blocks[j]
                source = jnp.where(phase == 2, z[m, rows, :], turned[m, rows, :])
                z[m, rows, :] = unit_rows(dot3(split(source), (a_high[m], a_low[m])))

            def again(m, j):
                rows = blocks[j]
                once = z[m, rows, :]
                z[m, rows, :] = jnp.where(phase == 0, unit_rows(dot3(split(once), (a_high[m], a_low[m]))), once)

            def products(m, j):
                part = split(z[m, blocks[j], :])
                other = [tuple(rotated(x, m) for x in part)]
                if j:
                    other.append(tuple(rotated(x, m) for x in split(z[m, blocks[j - 1], :])))
                result = dot3(part, tuple(jnp.concatenate(x, axis=0) for x in zip(*other)), NT) if j else dot3_narrow(part, other[0])
                square[m] = result[:, :SUB]
                if j:
                    near[m] = result[:, SUB:]

            def couple(m, j):
                value = dot3_tile(split(near[m]), split(inverses[j - 1][m]), NT)
                near[m] = value
                value = split(value)
                square[m] -= dot3_tile(value, tuple(rotated(x, m) for x in value), NT)

            def project(m, j):
                z[m, blocks[j], :] -= dot3_deep(split(near[m]), split(z[m, blocks[j - 1], :]))

            def align(m, j, count):
                fixed = split(z[m, : count * SUB, :])
                part = split(z[m, blocks[j], :])
                if count == 1:
                    z[m, blocks[j], :] -= dot3_deep(split(dot3_narrow(part, fixed)), fixed)
                else:
                    z[m, blocks[j], :] -= dot3(split(dot3(part, fixed, NT)), fixed)

            def scale(m, j):
                part = tuple(rotated(x, m) for x in split(z[m, blocks[j], :]))
                z[m, blocks[j], :] = dot3_deep(split(inverses[j][m]), part)

            def turn_back(m, columns):
                fresh[m, :, columns] = z[m, columns, :].T

            def guarded(m, x):
                unit = jnp.where((lane + (SUB - m * LEAF)) % SUB == row, 1.0, 0.0)
                return jnp.where(wanted[m // SLOTS] != 0, x, unit)

            def every(cost, task, *more):
                return [(cost, functools.partial(task, m, *more)) for m in range(MATS)]

            def step_tasks(cost, stage):
                return [(cost, functools.partial(stage, s, rows)) for s in range(SLOTS) for rows in blocks]

            inverses = [None] * len(blocks)
            firsts, middles, backs, ends = (
                step_tasks(cost, stage) for cost, stage in ((2, first_product), (3, moments), (3, back), (3, finish))
            )
            windows = [
                every(3, power, 1) + every(3, again, 1) + every(1, products, 1) + every(3, power, 2) + every(3, again, 2) + firsts,
                every(1, scale, 0) + every(1, project, 1) + every(2, align, 2, 1) + every(1, products, 2)
                + every(3, power, 3) + every(3, again, 3) + middles[:4],
                every(1, scale, 1) + every(1, project, 2) + every(2, align, 3, 2) + every(1, products, 3) + middles[4:] + backs[:4],
                every(1, scale, 2) + every(1, project, 3) + backs[4:] + ends + every(2, turn_back, slice(0, 3 * SUB)),
            ]
            weights = LEAF_WEIGHTS * (SUB // LEAF)
            for m in range(MATS):
                power(m, 0)
            for m in range(MATS):
                again(m, 0)
            for m in range(MATS):
                products(m, 0)

            @pl.when(phase == 0)
            def _():
                wait_late()

            for j in range(len(blocks)):
                for m in range(MATS):
                    if j:
                        couple(m, j)
                    work[m] = guarded(m, square[m])
                factor(work, worst_ref, spread_out(windows[j], weights))
                inverses[j] = [work[m] for m in range(MATS)]
            for m in range(MATS):
                scale(m, len(blocks) - 1)
            bad = jnp.max(worst_ref[...]) > 0.5
            return phase + 1, jnp.where((phase == 0) & bad, 3, limit)

        lax.while_loop(lambda carry: carry[0] < carry[1], sweep, (jnp.int32(0), jnp.int32(1)))

    update_copy = pltpu.make_async_copy(update, update_out, out_sems.at[0])
    update_copy.start()
    for m in range(MATS):
        s, side = divmod(m, 2)
        target = (new_left, new_right)[side].at[s]
        semaphore = out_sems.at[1 + m]

        @pl.when(wanted[s] != 0)
        def _():
            fresh[m, :, blocks[-1]] = z[m, blocks[-1], :].T
            pltpu.make_async_copy(fresh.at[m], target, semaphore).start()


    update_copy.wait()
    for m in range(MATS):
        s, side = divmod(m, 2)
        pltpu.make_async_copy(fresh.at[m], (new_left, new_right)[side].at[s], out_sems.at[1 + m]).wait()


def pack_kernel(table, gradient, outbox):
    @pl.loop(0, outbox.shape[0])
    def _(k):
        start = pl.multiple_of(jnp.maximum(table[k], 0) * BLOCK, BLOCK)
        piece = gradient[:, pl.ds(start, BLOCK)]
        outbox[k] = jnp.where(table[k] >= 0, piece, jnp.zeros_like(piece))


def prepare(left, right):
    vmem = pl.BlockSpec(memory_space=pltpu.VMEM)
    short = pltpu.HBM((SLOTS, BLOCK, BLOCK), bf16)
    return pl.pallas_call(
        prepare_kernel,
        out_shape=(pltpu.HBM((MATS, BLOCK, BLOCK), f32), short, short),
        in_specs=[vmem, vmem],
        out_specs=(vmem,) * 3,
        compiler_params=pltpu.CompilerParams(vmem_limit_bytes=16 * 1024 * 1024),
        cost_estimate=pl.CostEstimate(flops=8_000_000, bytes_accessed=10 * 1024 * 1024, transcendentals=0),
    )(*(pltpu.with_memory_space_constraint(x, pltpu.HBM) for x in (left, right)))


def step(held, wanted, grads, first, second, left_gram, right_gram, left, right):
    anywhere = pl.BlockSpec(memory_space=pl.ANY)
    smem = pl.BlockSpec(memory_space=pltpu.SMEM)
    whole = jax.ShapeDtypeStruct((SLOTS, BLOCK, BLOCK), f32)
    turned, right_high, right_low = prepare(left, right)
    large = (grads, turned, left, right_high, right_low, left_gram, right_gram, first, second, right)
    pair = pltpu.VMEM((SLOTS, BLOCK, BLOCK), f32)
    short_pair = pltpu.VMEM((SLOTS, BLOCK, BLOCK), bf16)
    four = pltpu.VMEM((MATS, BLOCK, BLOCK), f32)
    short_four = pltpu.VMEM((MATS, BLOCK, BLOCK), bf16)
    small = pltpu.VMEM((MATS, SUB, SUB), f32)
    return pl.pallas_call(
        step_kernel,
        out_shape=(whole, whole, whole),
        in_specs=[smem, smem] + [anywhere] * len(large),
        out_specs=(anywhere, anywhere, anywhere),
        scratch_shapes=[
            pltpu.VMEM((SLOTS, *grads.shape[:1], *grads.shape[2:]), bf16),
            four, pair, short_pair, short_pair, pair, pair, pair, pair,
            pair, pair, four, short_four, short_four, small, small, small, four,
            pltpu.VMEM((1, 128), f32),
            pltpu.SemaphoreType.DMA((3 * SLOTS + 6,)),
            pltpu.SemaphoreType.DMA((1 + MATS,)),
        ],
        compiler_params=pltpu.CompilerParams(vmem_limit_bytes=52 * 1024 * 1024),
    )(held, wanted, *(pltpu.with_memory_space_constraint(x, pltpu.HBM) for x in large))


def local(
    gradient, slot_block, refresh_target, first_moment, second_moment, left_gram, right_gram, left_basis, right_basis
):
    owners = lax.axis_size("dp")
    owner = lax.axis_index("dp")
    device = owner * lax.axis_size("tensor") + lax.axis_index("tensor")
    table = slot_block[0]
    slab = gradient.shape[2]
    vmem = pl.BlockSpec(memory_space=pltpu.VMEM)
    smem = pl.BlockSpec(memory_space=pltpu.SMEM)
    outbox = pl.pallas_call(
        pack_kernel,
        out_shape=jax.ShapeDtypeStruct((owners * SLOTS, slab, BLOCK), bf16),
        in_specs=[smem, vmem],
        out_specs=vmem,
    )(table, gradient[0, 0])
    grads = lax.all_to_all(outbox.reshape(owners, SLOTS, slab, BLOCK), "dp", 0, 0, tiled=True)
    held = (lax.dynamic_slice_in_dim(table, owner * SLOTS, SLOTS) >= 0).astype(jnp.int32)
    wanted = (lax.dynamic_slice_in_dim(refresh_target, device * SLOTS, SLOTS) >= 0).astype(jnp.int32)
    outputs = step(
        held, wanted, grads, first_moment[0], second_moment[0], left_gram[0], right_gram[0], left_basis[0], right_basis[0]
    )
    return tuple(x[None] for x in outputs)


def solution(mesh):
    rows = P("tensor", "dp", None, None)
    return jax.shard_map(
        local,
        mesh=mesh,
        in_specs=(P("tensor", None, "dp", None), P("tensor", None), P(), rows, rows, rows, rows, rows, rows),
        out_specs=(rows, rows, rows),
        check_vma=False,
    )
```

```python
import functools

import jax
import jax.numpy as jnp
from jax import lax
from jax.experimental import pallas as pl
from jax.experimental.pallas import tpu as pltpu
from jax.sharding import PartitionSpec as P

BLOCK = 512
SUB = 128
LEAF = 32
SLOTS = 2
MATS = 2 * SLOTS
CHUNK = 256
WORST = 10.0
LEAF_WEIGHTS = [2, 2, 2, 2, 2, 2]

f32 = jnp.float32
bf16 = jnp.bfloat16

NN = (((1,), (0,)), ((), ()))
NT = (((1,), (1,)), ((), ()))
TN = (((0,), (0,)), ((), ()))


def split(x):
    high = x.astype(bf16)
    return high, (x - high.astype(f32)).astype(bf16)


def dot(a, b, dims=NN):
    return lax.dot_general(a, b, dims, preferred_element_type=f32)


def dot3(a, b, dims=NN):
    return dot(a[0], b[0], dims) + (dot(a[0], b[1], dims) + dot(a[1], b[0], dims))


def dot3_tile(a, b, dims=NN):
    zeros = jnp.zeros((SUB, SUB), bf16)
    if dims == NN:
        top, bottom = (b[0], b[1]), (b[0], zeros)
    else:
        top, bottom = (b[0], b[0]), (b[1], zeros)
    operand = jnp.concatenate([jnp.concatenate(top, axis=1), jnp.concatenate(bottom, axis=1)], axis=0)
    result = dot(jnp.concatenate(a, axis=1), operand, dims)
    return result[:, :SUB] + result[:, SUB:]


def dot3_deep(a, b):
    return dot(jnp.concatenate(a, axis=1), jnp.concatenate([b[0], b[0]], axis=0)) + dot(a[0], b[1])


def dot3_narrow(a, b):
    result = dot(a[0], jnp.concatenate(b, axis=0), NT)
    return result[:, :SUB] + (result[:, SUB:] + dot(a[1], b[0], NT))


def unit_rows(x):
    return x * lax.rsqrt(jnp.sum(x * x, axis=1, keepdims=True))


def leaf(tiles, hooks):
    lane = lax.broadcasted_iota(jnp.int32, (8, 128), 1)
    row = lax.broadcasted_iota(jnp.int32, (8, 128), 0)
    within = lane % LEAF
    base = lane - within
    worst = jnp.zeros((1, 128), f32)
    tiles = list(tiles)
    depth = LEAF // 8
    pick = lambda t, j: jnp.take_along_axis(tiles[t], base + j, axis=1)
    columns = [[pick(t, q) for t in range(depth)] for q in range(8)]
    for t0 in range(depth):
        ahead = [[pick(t, 8 * t0 + 8 + q) for t in range(t0 + 1, depth)] for q in range(8)] if t0 + 1 < depth else []
        for q in range(8):
            inverse = lax.rsqrt(columns[q][0][q : q + 1, :])
            worst = jnp.maximum(worst, jnp.where(inverse < WORST, 0.0, 1.0))
            factors = [column * inverse for column in columns[q]]
            factors[0] = jnp.where(row > q, factors[0], 0.0)
            for r in range(q + 1, 8):
                across = factors[0][r : r + 1, :]
                columns[r] = [column - factor * across for column, factor in zip(columns[r], factors)]
            here = within[:1] == 8 * t0 + q
            scaled = (tiles[t0][q : q + 1, :] + jnp.where(here, 1.0, 0.0)) * inverse
            for t in range(t0, depth):
                tiles[t] = tiles[t] - factors[t - t0] * scaled
            tiles[t0] = jnp.where(row == q, jnp.where(here, inverse, scaled), tiles[t0])
            for r in range(8 if ahead else 0):
                across = factors[1][r : r + 1, :]
                ahead[r] = [column - factor * across for column, factor in zip(ahead[r], factors[1:])]
        columns = ahead
        hooks[t0]()
    for t in range(LEAF // 8):
        tiles[t] = jnp.where(within <= row + 8 * t, tiles[t], 0.0)
    return tiles, worst


def rotated(x, m):
    cut = SUB - m * LEAF
    return x if m == 0 else jnp.concatenate([x[cut:], x[:cut]], axis=0)


def factor(work, worst_ref, tasks):
    lane = lax.broadcasted_iota(jnp.int32, (SUB, SUB), 1)
    row = lax.broadcasted_iota(jnp.int32, (SUB, SUB), 0)
    group = lane // LEAF
    own = group == row // LEAF
    steps = SUB // LEAF
    current = [work[m, :LEAF, :] for m in range(MATS)]
    for b in range(steps):
        rows = slice(b * LEAF, (b + 1) * LEAF)
        stacked = jnp.concatenate([current[(g - b) % MATS] for g in range(MATS)], axis=0)
        packed = stacked[:LEAF]
        for g in range(1, MATS):
            packed = jnp.where(group[:LEAF] == g, stacked[g * LEAF : (g + 1) * LEAF], packed)
        tiles, worst = leaf([packed[8 * t : 8 * t + 8] for t in range(LEAF // 8)], tasks[6 * b : 6 * b + 4])
        worst_ref[...] = jnp.maximum(worst_ref[...], worst)
        inverse = jnp.where(own, jnp.concatenate(tiles * MATS, axis=0), 0.0)
        pair = split(inverse)

        height = SUB - (b + 2) * LEAF
        if b + 1 < steps:
            following = slice((b + 1) * LEAF, (b + 2) * LEAF)
            pieces = [(m, following, LEAF) for m in range(MATS)]
            if height:
                pieces += [(m, slice((b + 2) * LEAF, SUB), height) for m in range(MATS)]
            old = jnp.concatenate([work[m, under, :] for m, under, _ in pieces], axis=0)
            mine = jnp.concatenate([group[:size] == (b + m) % MATS for m, _, size in pieces], axis=0)
            factors = jnp.where(mine, dot3_tile(split(old), pair, NT), 0.0)
        band = jnp.where(own, inverse, dot3_tile(pair, split(stacked)))
        tasks[6 * b + 4]()
        if b + 1 < steps:
            fresh = jnp.where(mine, 0.0, old) - dot3_tile(split(factors), split(band))
            current = [fresh[m * LEAF : (m + 1) * LEAF] for m in range(MATS)]
            for m in range(MATS if height else 0):
                start = MATS * LEAF + m * height
                work[m, (b + 2) * LEAF :, :] = fresh[start : start + height]
        tasks[6 * b + 5]()
        for g in range(MATS):
            work[(g - b) % MATS, rows, :] = band[g * LEAF : (g + 1) * LEAF]
    for m in range(MATS):
        column = (lane + (SUB - m * LEAF)) % SUB
        work[m] = jnp.where(column <= row, work[m], 0.0)


def spread_out(tasks, weights):
    total = sum(cost for cost, _ in tasks)
    edges = [total * sum(weights[: i + 1]) / sum(weights) for i in range(len(weights))]
    shares = [[] for _ in weights]
    done = 0.0
    at = 0
    for cost, call in tasks:
        while at + 1 < len(weights) and done + cost / 2 > edges[at]:
            at += 1
        shares[at].append(call)
        done += cost

    def run(calls):
        for call in calls:
            call()

    return [functools.partial(run, calls) for calls in shares]


def prepare_kernel(left, right, turned, right_high, right_low):
    for s in range(SLOTS):
        turned[2 * s] = left[s].T
        turned[2 * s + 1] = right[s].T
        right_high[s], right_low[s] = split(right[s])


def step_kernel(
    held, wanted, grads, turned_in, left_in, right_high_in, right_low_in, left_gram_in, right_gram_in, first_in, second_in, right_in,
    update_out, new_left, new_right,
    g, turned, left, right, right_high, right_low, left_gram, right_gram, first, second,
    update, temp, z, a_high, a_low, work, near, square, fresh, worst_ref, in_sems, out_sems,
):
    halves = [slice(c, c + CHUNK) for c in range(0, BLOCK, CHUNK)]
    blocks = [slice(c, c + SUB) for c in range(0, BLOCK, SUB)]
    used = []

    def copy_in(source, target):
        used.append(pltpu.make_async_copy(source, target, in_sems.at[len(used)]))
        return used[-1]

    early = [
        [
            copy_in(grads.at[:, s], g.at[s]),
            copy_in(left_gram_in.at[s], left_gram.at[s]),
            copy_in(right_gram_in.at[s], right_gram.at[s]),
        ]
        for s in range(SLOTS)
    ]
    middle = copy_in(turned_in, turned)
    late = [
        copy_in(source, target)
        for source, target in (
            (right_high_in, right_high),
            (right_low_in, right_low),
            (first_in, first),
            (second_in, second),
            (left_in, left),
            (right_in, right),
        )
    ]
    for copies in early:
        for copy in copies:
            copy.start()
    middle.start()
    for copy in early[0]:
        copy.wait()
    for copy in late:
        copy.start()

    def wait_late():
        for copy in late:
            copy.wait()

    def g_block(s):
        return g[s].reshape(BLOCK, BLOCK)

    def right_pair(s):
        return right_high[s], right_low[s]

    def first_product(s, rows):
        high, low = split(turned[2 * s, rows, :])
        temp[s, rows, :] = dot(high, g_block(s)) + dot(low, g_block(s))

    def moments(s, rows):
        rotated_rows = dot3(split(temp[s, rows, :]), right_pair(s))
        moment = 0.9 * first[s, rows, :] + 0.1 * rotated_rows
        spread = 0.95 * second[s, rows, :] + 0.05 * rotated_rows * rotated_rows
        temp[s, rows, :] = moment / (jnp.sqrt(spread) + 1e-08)

    def back(s, rows):
        update[s, rows, :] = dot3(split(left[s, rows, :]), split(temp[s]))

    def finish(s, rows):
        result = dot3(split(update[s, rows, :]), right_pair(s), NT)
        update[s, rows, :] = jnp.where(held[s] != 0, result, 0.0)

    refresh = (wanted[0] + wanted[1]) != 0

    @pl.when(jnp.logical_not(refresh))
    def _():
        for copy in early[1]:
            copy.wait()
        middle.wait()
        wait_late()

        @pl.loop(0, SLOTS)
        def _(s):
            @pl.when(held[s] == 0)
            def _():
                update[s] = jnp.zeros((BLOCK, BLOCK), f32)

            @pl.when(held[s] != 0)
            def _():
                for stage in (first_product, moments, back, finish):
                    for rows in halves:
                        stage(s, rows)

    @pl.when(refresh)
    def _():
        for s in range(SLOTS):
            if s:
                for copy in early[s]:
                    copy.wait()
            gs = g_block(s)
            gt = gs.T
            for side in range(2):
                m = SLOTS * s + side
                for rows in halves:
                    pieces = (gs[rows], gs, NT) if side == 0 else (gt[rows], gs, NN)
                    past = (left_gram, right_gram)[side][s, rows, :]
                    a_high[m, rows, :], a_low[m, rows, :] = split(0.95 * past + 0.05 * dot(*pieces))

        middle.wait()

        def sweep(carry):
            phase, limit = carry
            worst_ref[...] = jnp.zeros((1, 128), f32)
            lane = lax.broadcasted_iota(jnp.int32, (SUB, SUB), 1)
            row = lax.broadcasted_iota(jnp.int32, (SUB, SUB), 0)

            def power(m, j):
                rows = blocks[j]
                source = jnp.where(phase == 2, z[m, rows, :], turned[m, rows, :])
                z[m, rows, :] = unit_rows(dot3(split(source), (a_high[m], a_low[m])))

            def again(m, j):
                rows = blocks[j]
                once = z[m, rows, :]
                z[m, rows, :] = jnp.where(phase == 0, unit_rows(dot3(split(once), (a_high[m], a_low[m]))), once)

            def products(m, j):
                part = split(z[m, blocks[j], :])
                other = [tuple(rotated(x, m) for x in part)]
                if j:
                    other.append(tuple(rotated(x, m) for x in split(z[m, blocks[j - 1], :])))
                result = dot3(part, tuple(jnp.concatenate(x, axis=0) for x in zip(*other)), NT) if j else dot3_narrow(part, other[0])
                square[m] = result[:, :SUB]
                if j:
                    near[m] = result[:, SUB:]

            def couple(m, j):
                value = dot3_tile(split(near[m]), split(inverses[j - 1][m]), NT)
                near[m] = value
                value = split(value)
                square[m] -= dot3_tile(value, tuple(rotated(x, m) for x in value), NT)

            def project(m, j):
                z[m, blocks[j], :] -= dot3_deep(split(near[m]), split(z[m, blocks[j - 1], :]))

            def align(m, j, count):
                fixed = split(z[m, : count * SUB, :])
                part = split(z[m, blocks[j], :])
                if count == 1:
                    z[m, blocks[j], :] -= dot3_deep(split(dot3_narrow(part, fixed)), fixed)
                else:
                    z[m, blocks[j], :] -= dot3(split(dot3(part, fixed, NT)), fixed)

            def scale(m, j):
                part = tuple(rotated(x, m) for x in split(z[m, blocks[j], :]))
                z[m, blocks[j], :] = dot3_deep(split(inverses[j][m]), part)

            def turn_back(m, columns):
                fresh[m, :, columns] = z[m, columns, :].T

            def guarded(m, x):
                unit = jnp.where((lane + (SUB - m * LEAF)) % SUB == row, 1.0, 0.0)
                return jnp.where(wanted[m // SLOTS] != 0, x, unit)

            def every(cost, task, *more):
                return [(cost, functools.partial(task, m, *more)) for m in range(MATS)]

            def step_tasks(cost, stage):
                return [(cost, functools.partial(stage, s, rows)) for s in range(SLOTS) for rows in blocks]

            inverses = [None] * len(blocks)
            firsts, middles, backs, ends = (
                step_tasks(cost, stage) for cost, stage in ((2, first_product), (3, moments), (3, back), (3, finish))
            )
            windows = [
                every(3, power, 1) + every(3, again, 1) + every(1, products, 1) + every(3, power, 2) + every(3, again, 2) + firsts,
                every(1, scale, 0) + every(1, project, 1) + every(2, align, 2, 1) + every(1, products, 2)
                + every(3, power, 3) + every(3, again, 3) + middles[:4],
                every(1, scale, 1) + every(1, project, 2) + every(2, align, 3, 2) + every(1, products, 3) + middles[4:] + backs[:4],
                every(1, scale, 2) + every(1, project, 3) + backs[4:] + ends + every(2, turn_back, slice(0, 3 * SUB)),
            ]
            weights = LEAF_WEIGHTS * (SUB // LEAF)
            for m in range(MATS):
                power(m, 0)
            for m in range(MATS):
                again(m, 0)
            for m in range(MATS):
                products(m, 0)

            @pl.when(phase == 0)
            def _():
                wait_late()

            for j in range(len(blocks)):
                for m in range(MATS):
                    if j:
                        couple(m, j)
                    work[m] = guarded(m, square[m])
                factor(work, worst_ref, spread_out(windows[j], weights))
                inverses[j] = [work[m] for m in range(MATS)]
            for m in range(MATS):
                scale(m, len(blocks) - 1)
            bad = jnp.max(worst_ref[...]) > 0.5
            return phase + 1, jnp.where((phase == 0) & bad, 3, limit)

        lax.while_loop(lambda carry: carry[0] < carry[1], sweep, (jnp.int32(0), jnp.int32(1)))

    update_copy = pltpu.make_async_copy(update, update_out, out_sems.at[0])
    update_copy.start()
    for m in range(MATS):
        s, side = divmod(m, 2)
        target = (new_left, new_right)[side].at[s]
        semaphore = out_sems.at[1 + m]

        @pl.when(wanted[s] != 0)
        def _():
            fresh[m, :, blocks[-1]] = z[m, blocks[-1], :].T
            pltpu.make_async_copy(fresh.at[m], target, semaphore).start()

        @pl.when(wanted[s] == 0)
        def _():
            pltpu.make_async_copy((left, right)[side].at[s], target, semaphore).start()


    update_copy.wait()
    for m in range(MATS):
        s, side = divmod(m, 2)
        pltpu.make_async_copy(fresh.at[m], (new_left, new_right)[side].at[s], out_sems.at[1 + m]).wait()


def pack_kernel(table, gradient, outbox):
    @pl.loop(0, outbox.shape[0])
    def _(k):
        start = pl.multiple_of(jnp.maximum(table[k], 0) * BLOCK, BLOCK)
        piece = gradient[:, pl.ds(start, BLOCK)]
        outbox[k] = jnp.where(table[k] >= 0, piece, jnp.zeros_like(piece))


def prepare(left, right):
    vmem = pl.BlockSpec(memory_space=pltpu.VMEM)
    short = pltpu.HBM((SLOTS, BLOCK, BLOCK), bf16)
    return pl.pallas_call(
        prepare_kernel,
        out_shape=(pltpu.HBM((MATS, BLOCK, BLOCK), f32), short, short),
        in_specs=[vmem, vmem],
        out_specs=(vmem,) * 3,
        compiler_params=pltpu.CompilerParams(vmem_limit_bytes=16 * 1024 * 1024),
        cost_estimate=pl.CostEstimate(flops=8_000_000, bytes_accessed=10 * 1024 * 1024, transcendentals=0),
    )(*(pltpu.with_memory_space_constraint(x, pltpu.HBM) for x in (left, right)))


def step(held, wanted, grads, first, second, left_gram, right_gram, left, right):
    anywhere = pl.BlockSpec(memory_space=pl.ANY)
    smem = pl.BlockSpec(memory_space=pltpu.SMEM)
    whole = jax.ShapeDtypeStruct((SLOTS, BLOCK, BLOCK), f32)
    turned, right_high, right_low = prepare(left, right)
    large = (turned, left, right_high, right_low, left_gram, right_gram, first, second, right)
    pair = pltpu.VMEM((SLOTS, BLOCK, BLOCK), f32)
    short_pair = pltpu.VMEM((SLOTS, BLOCK, BLOCK), bf16)
    four = pltpu.VMEM((MATS, BLOCK, BLOCK), f32)
    short_four = pltpu.VMEM((MATS, BLOCK, BLOCK), bf16)
    small = pltpu.VMEM((MATS, SUB, SUB), f32)
    return pl.pallas_call(
        step_kernel,
        out_shape=(whole, whole, whole),
        in_specs=[smem, smem, anywhere] + [anywhere] * len(large),
        out_specs=(anywhere, anywhere, anywhere),
        scratch_shapes=[
            pltpu.VMEM((SLOTS, *grads.shape[:1], *grads.shape[2:]), bf16),
            four, pair, pair, short_pair, short_pair, pair, pair, pair, pair,
            pair, pair, four, short_four, short_four, small, small, small, four,
            pltpu.VMEM((1, 128), f32),
            pltpu.SemaphoreType.DMA((3 * SLOTS + 7,)),
            pltpu.SemaphoreType.DMA((1 + MATS,)),
        ],
        compiler_params=pltpu.CompilerParams(vmem_limit_bytes=52 * 1024 * 1024),
    )(held, wanted, grads, *(pltpu.with_memory_space_constraint(x, pltpu.HBM) for x in large))


def local(
    gradient, slot_block, refresh_target, first_moment, second_moment, left_gram, right_gram, left_basis, right_basis
):
    owners = lax.axis_size("dp")
    owner = lax.axis_index("dp")
    device = owner * lax.axis_size("tensor") + lax.axis_index("tensor")
    table = slot_block[0]
    slab = gradient.shape[2]
    vmem = pl.BlockSpec(memory_space=pltpu.VMEM)
    smem = pl.BlockSpec(memory_space=pltpu.SMEM)
    outbox = pl.pallas_call(
        pack_kernel,
        out_shape=jax.ShapeDtypeStruct((owners * SLOTS, slab, BLOCK), bf16),
        in_specs=[smem, vmem],
        out_specs=vmem,
    )(table, gradient[0, 0])
    grads = lax.all_to_all(outbox.reshape(owners, SLOTS, slab, BLOCK), "dp", 0, 0, tiled=True)
    held = (lax.dynamic_slice_in_dim(table, owner * SLOTS, SLOTS) >= 0).astype(jnp.int32)
    wanted = (lax.dynamic_slice_in_dim(refresh_target, device * SLOTS, SLOTS) >= 0).astype(jnp.int32)
    outputs = step(
        held, wanted, grads, first_moment[0], second_moment[0], left_gram[0], right_gram[0], left_basis[0], right_basis[0]
    )
    return tuple(x[None] for x in outputs)


def solution(mesh):
    rows = P("tensor", "dp", None, None)
    return jax.shard_map(
        local,
        mesh=mesh,
        in_specs=(P("tensor", None, "dp", None), P("tensor", None), P(), rows, rows, rows, rows, rows, rows),
        out_specs=(rows, rows, rows),
        check_vma=False,
    )
```
